512 devices in a mesh: dp: 16 (over y, core), prec: 32 (over x, z).
Axes of the slice: x: 4, y: 8, z: 8, core: 2. Of those that a mesh axis runs over, the one named last changes fastest.
Arguments:
- grad_part: bfloat16 [16, 40, 16, 32, 2, 1024], P('dp', None, None, 'prec')
- table: int32 [40], replicated, may hold values from 0 to 95, as said below
- left_root: bfloat16 [96, 1024, 1024], P('prec', 'dp'), as said below
- right_root: bfloat16 [96, 1024, 1024], P('prec', 'dp'), as said below
Outputs:
- left_gram_stats: float32 [96, 1024, 1024], P('prec', 'dp')
- right_gram_stats: float32 [96, 1024, 1024], P('prec', 'dp')
- update: bfloat16 [40, 16, 32, 2, 1024], P(None, 'dp', 'prec')
The draws below stay inside these ranges and needn't reach their ends.
Inputs may be any that keep to these rules, and one draw needn't show every extreme that they name: `table`: the 40 entries are distinct slots; slot s belongs to owner s // 3 of prec; in every draw some owner holds 3 blocks, and slots 0 and 95 are used. `left_root`: symmetric. `right_root`: symmetric.
All inputs are finite; a program needn't handle non-finite values.
Results may differ from the reference program's by a relative error of at most 0.018.
Values may be sent and summed in bfloat16 or wider, within the bound.
A program may use at most 64 MiB of HBM per device.

```python
import math
import jax
import jax.numpy as jnp
from jax import lax

BLOCK_ORDER = 1024
OWNER_SLOTS = 3
SLOT_TOTAL = 96
NB = 40
RSUB = 2
N_DP = 16
N_PREC = 32


def draw_grad_part(key, part):
    key = jax.random.fold_in(key, 11)
    key_rows = jax.random.fold_in(key, 0)
    key_cols = jax.random.fold_in(key, 1)
    key_noise = jax.random.fold_in(key, 2)
    key_left = jax.random.fold_in(key, 4)
    key_right = jax.random.fold_in(key, 5)
    position = jnp.arange(BLOCK_ORDER, dtype=jnp.float32).reshape(1, BLOCK_ORDER, 1) / BLOCK_ORDER
    rise = math.log(5.0)
    lift = 0.7 / math.sqrt(N_DP)
    rows = jnp.exp(position * rise + jax.random.uniform(key_rows, (NB, BLOCK_ORDER, 1), jnp.float32, 0.0, math.log(2.0)))
    cols = jnp.exp(jax.random.uniform(key_cols, (NB, 1, BLOCK_ORDER), jnp.float32, 0.0, math.log(10.0)))
    left_vector = jax.random.uniform(key_left, (NB, BLOCK_ORDER, 1), jnp.float32, 0.5, 1.0)
    right_vector = jax.random.uniform(key_right, (NB, 1, BLOCK_ORDER), jnp.float32, 0.5, 1.0)
    noise_term = jax.random.normal(key_noise, (N_DP, NB, BLOCK_ORDER, BLOCK_ORDER), jnp.float32)
    values = 0.06 * (noise_term + lift * left_vector * right_vector) * rows * cols
    return values.reshape(N_DP, NB, N_DP, N_PREC, RSUB, BLOCK_ORDER).astype(jnp.bfloat16)


def draw_table(key, part):
    key = jax.random.fold_in(key, 23)
    key_ranking, key_owner, key_order = jax.random.split(key, 3)
    rank_values = jax.random.permutation(key_ranking, SLOT_TOTAL).astype(jnp.int32)
    owner_index = jax.random.randint(key_owner, (), 0, N_PREC).astype(jnp.int32)
    slot_index = jnp.arange(SLOT_TOTAL, dtype=jnp.int32)
    forced_choice = (slot_index // OWNER_SLOTS == owner_index) | (slot_index == 0) | (slot_index == SLOT_TOTAL - 1)
    priority_score = rank_values + SLOT_TOTAL * forced_choice.astype(jnp.int32)
    chosen = jnp.argsort(-priority_score)[:NB].astype(jnp.int32)
    shuffle = jax.random.permutation(key_order, NB)
    return chosen[shuffle].astype(jnp.int32)


def symmetric_root(key, diagonal_part, fall):
    key_noise, key_vector = jax.random.split(key)
    off_noise = jax.random.normal(key_noise, (SLOT_TOTAL, BLOCK_ORDER, BLOCK_ORDER), jnp.float32)
    off_part = 0.155 / math.sqrt(BLOCK_ORDER) * (off_noise + jnp.swapaxes(off_noise, 1, 2))
    smooth_vector = jax.random.uniform(key_vector, (SLOT_TOTAL, BLOCK_ORDER), jnp.float32, 0.5, 1.0)
    smooth_part = 2.0 / BLOCK_ORDER * smooth_vector[:, :, None] * smooth_vector[:, None, :]
    eye = jnp.eye(BLOCK_ORDER, dtype=jnp.float32)
    core = (off_part + smooth_part) * (1.0 - eye) + eye * diagonal_part[:, :, None]
    position = jnp.arange(BLOCK_ORDER, dtype=jnp.float32) / BLOCK_ORDER
    side = jnp.exp(-0.5 * fall * position)
    return side[None, :, None] * core * side[None, None, :]


def draw_left_root(key, part):
    key = jax.random.fold_in(key, 37)
    key_diagonal, key_offdiagonal = jax.random.split(key)
    diagonal_part = jnp.exp(jax.random.uniform(key_diagonal, (SLOT_TOTAL, BLOCK_ORDER), jnp.float32, math.log(0.5), math.log(2.0)))
    return symmetric_root(key_offdiagonal, diagonal_part, math.log(5.0)).astype(jnp.bfloat16)


def draw_right_root(key, part):
    key = jax.random.fold_in(key, 41)
    key_diagonal, key_offdiagonal = jax.random.split(key)
    diagonal_part = jnp.exp(jax.random.uniform(key_diagonal, (SLOT_TOTAL, BLOCK_ORDER), jnp.float32, math.log(0.5), math.log(2.0)))
    return symmetric_root(key_offdiagonal, diagonal_part, 0.0).astype(jnp.bfloat16)


def setup_inputs(seed: int = 0) -> dict:
    seeds = jax.random.split(jax.random.key(seed), 5)
    grad_part = draw_grad_part(jax.random.fold_in(seeds[4], 71), 0)
    table = draw_table(jax.random.fold_in(seeds[4], 71), 0)
    left_root = draw_left_root(jax.random.fold_in(seeds[4], 71), 0)
    right_root = draw_right_root(jax.random.fold_in(seeds[4], 71), 0)
    return {"grad_part": grad_part, "table": table, "left_root": left_root, "right_root": right_root}


def one_block(inputs):
    block, left, right = inputs
    left_statistic = jnp.dot(block, block.T, preferred_element_type=jnp.float32)
    right_statistic = jnp.dot(block.T, block, preferred_element_type=jnp.float32)
    half = jnp.dot(left, block, preferred_element_type=jnp.float32).astype(jnp.bfloat16)
    precond = jnp.dot(half, right, preferred_element_type=jnp.float32)
    grad_norm = jnp.sqrt(jnp.sum(jnp.square(block.astype(jnp.float32))))
    prec_norm = jnp.sqrt(jnp.sum(precond * precond))
    grafted = (precond * (grad_norm / (prec_norm + 1e-06))).astype(jnp.bfloat16)
    return (left_statistic, right_statistic, grafted)

def reference(grad_part, table, left_root, right_root):
    gradient = lax.optimization_barrier(jnp.sum(grad_part, axis=0, dtype=jnp.float32)).astype(jnp.bfloat16)
    blocks = gradient.reshape(NB, BLOCK_ORDER, BLOCK_ORDER)
    lefts = jnp.take(left_root, table, axis=0)
    rights = jnp.take(right_root, table, axis=0)
    left_statistic, right_statistic, grafted = lax.map(one_block, (blocks, lefts, rights))
    left_gram_stats = jnp.zeros((SLOT_TOTAL, BLOCK_ORDER, BLOCK_ORDER), jnp.float32).at[table].set(left_statistic)
    right_gram_stats = jnp.zeros((SLOT_TOTAL, BLOCK_ORDER, BLOCK_ORDER), jnp.float32).at[table].set(right_statistic)
    update = grafted.reshape(NB, N_DP, N_PREC, RSUB, BLOCK_ORDER)
    return (left_gram_stats, right_gram_stats, update)
```

```python
import jax
import jax.numpy as jnp
from jax import lax
from jax.experimental import pallas as pl
from jax.experimental.pallas import tpu as pltpu
from jax.sharding import PartitionSpec as P

MESH = pl.DeviceIdType.MESH
BF = jnp.bfloat16
F32 = jnp.float32

NY = 8
NDP = 16
NPREC = 32
SL = 3
NB = 40
STRIP = 64
ORDER = 1024
LANES = 128
Q = 16
HALF = NB // 2
SUB = HALF // 2
WIN = 5
TILE = 256
SIGNS = (1, -1)


def kernel(
    inv, table, grad, lroot, rroot, left_hbm, right_hbm, upd_hbm,
    part, sib, ringbuf, summed, slots, got, strip_t, strip_m, gall, wall, rfull,
    half_acc, half, prec_m, outgo, back, norm, norms, left_out, right_out, upd_out,
    part_sem, sib_s, sib_r, rs_s, rs_r, b_s, b_r,
    rr_s, rr_r, rd_s, rd_r, gr_s, gr_r, gd_s, gd_r,
    e_s, e_r, n_s, n_r, out_sem,
):
    d = lax.axis_index("dp")
    p = lax.axis_index("prec")
    y = d // 2
    core = d % 2
    other = 2 * y + (1 - core)

    def wrap(v):
        return (v + 4 * NY) % NY

    def dp_of(chip_y):
        return 2 * chip_y + core

    barrier = pltpu.get_barrier_semaphore()

    @pl.loop(1, NDP)
    def _(i):
        pl.semaphore_signal(barrier, inc=1, device_id=((d + i) % NDP, p), device_id_type=MESH)

    @pl.loop(1, NPREC)
    def _(i):
        pl.semaphore_signal(barrier, inc=1, device_id=(d, (p + i) % NPREC), device_id_type=MESH)

    def local_part(g, t):
        c = wrap(y - SIGNS[g] * (1 + t))
        blocks = pl.ds(g * HALF, HALF)
        return pltpu.make_async_copy(
            grad.at[blocks, 2 * c + core], part.at[c, blocks], part_sem.at[g, t]
        )

    def sib_part(g, t):
        c = wrap(y - SIGNS[g] * (1 + t))
        blocks = pl.ds(g * HALF, HALF)
        return pltpu.make_async_remote_copy(
            src_ref=grad.at[blocks, 2 * c + (1 - core)],
            dst_ref=sib.at[c, blocks],
            send_sem=sib_s.at[g, t],
            recv_sem=sib_r.at[g, t],
            device_id=(other, p),
            device_id_type=MESH,
        )

    for t in range(NY):
        for g in range(2):
            local_part(g, t).start()
    for w in range(WIN):
        cols = pl.ds(pl.multiple_of(wrap(y + w) * LANES, LANES), LANES)
        for s in range(SL):
            wall[s, d, :, w * LANES : (w + 1) * LANES] = rroot[s, :, cols]

    pl.semaphore_wait(barrier, NDP + NPREC - 2)
    for t in range(NY):
        for g in range(2):
            sib_part(g, t).start()

    def hop(buf, ss, rs, s, g, k):
        o = wrap(y - SIGNS[g] * (k - 1))
        rows = pl.ds(0, STRIP) if k < 4 else pl.ds(g * (STRIP // 2), STRIP // 2)
        ref = buf.at[s, dp_of(o), rows]
        return pltpu.make_async_remote_copy(
            src_ref=ref,
            dst_ref=ref,
            send_sem=ss.at[s, g, k - 1],
            recv_sem=rs.at[s, g, k - 1],
            device_id=(dp_of(wrap(y + SIGNS[g])), p),
            device_id_type=MESH,
        )

    def landing(buf, ss, rs, s, g, k):
        o = wrap(y - SIGNS[g] * k)
        rows = pl.ds(0, STRIP) if k < 4 else pl.ds(g * (STRIP // 2), STRIP // 2)
        ref = buf.at[s, dp_of(o), rows]
        return pltpu.make_async_remote_copy(
            src_ref=ref,
            dst_ref=ref,
            send_sem=ss.at[s, g, k - 1],
            recv_sem=rs.at[s, g, k - 1],
            device_id=(dp_of(wrap(y + SIGNS[g])), p),
            device_id_type=MESH,
        )

    def across(buf, ss, rs, s, g, k, mine):
        o = wrap(y - SIGNS[g] * k)
        rows = pl.ds(0, STRIP) if k < 4 else pl.ds(g * (STRIP // 2), STRIP // 2)
        ref = buf.at[s, 2 * o + (core if mine else 1 - core), rows]
        n = 0 if k == 0 else 1 + g * 4 + (k - 1)
        return pltpu.make_async_remote_copy(
            src_ref=ref,
            dst_ref=ref,
            send_sem=ss.at[s, n],
            recv_sem=rs.at[s, n],
            device_id=(other, p),
            device_id_type=MESH,
        )

    def ring_start(buf, rsem, dsem, s):
        for g in range(2):
            hop(buf, *rsem, s, g, 1).start()
        across(buf, *dsem, s, 0, 0, True).start()

    def ring_step(buf, rsem, dsem, s, k):
        for g in range(2):
            landing(buf, *rsem, s, g, k).wait_recv()
            if k < 4:
                hop(buf, *rsem, s, g, k + 1).start()
            across(buf, *dsem, s, g, k, True).start()

    def ring_other(buf, dsem, s, k):
        for g in range(2 if k else 1):
            across(buf, *dsem, s, g, k, False).wait_recv()

    def ring_drain(buf, rsem, dsem, s):
        for k in range(5):
            for g in range(2 if k else 1):
                if k:
                    hop(buf, *rsem, s, g, k).wait_send()
                across(buf, *dsem, s, g, k, True).wait_send()

    RR, RD, GR, GD = (rr_s, rr_r), (rd_s, rd_r), (gr_s, gr_r), (gd_s, gd_r)

    def rs_copy(g, t, u):
        c = wrap(y - SIGNS[g] * (1 + t))
        return pltpu.make_async_remote_copy(
            src_ref=part.at[c, pl.ds(g * HALF + u * SUB, SUB)],
            dst_ref=ringbuf.at[g, t, pl.ds(u * SUB, SUB)],
            send_sem=rs_s.at[g, t, u],
            recv_sem=rs_r.at[g, t, u],
            device_id=(dp_of(wrap(y + SIGNS[g])), p),
            device_id_type=MESH,
        )

    for t in range(NY):
        for u in range(2):
            for g in range(2):
                c = wrap(y - SIGNS[g] * (1 + t))
                if u == 0:
                    local_part(g, t).wait()
                    sib_part(g, t).wait_recv()
                blocks = pl.ds(g * HALF + u * SUB, SUB)
                total = part[c, blocks].astype(F32) + sib[c, blocks].astype(F32)
                if t > 0:
                    rs_copy(g, t - 1, u).wait_recv()
                    total += ringbuf[g, t - 1, pl.ds(u * SUB, SUB)].astype(F32)
                if t < NY - 1:
                    part[c, blocks] = total.astype(BF)
                    rs_copy(g, t, u).start()
                else:
                    summed[blocks] = total.astype(BF)
        if t in (1, 3, 5):
            ring_start(wall, RR, RD, t // 2)
        if t == 6:
            ring_step(wall, RR, RD, 0, 1)
    summed[NB] = jnp.zeros((Q, LANES), BF)

    @pl.loop(0, SL * NPREC, unroll=8)
    def _(s):
        slots[s] = summed[inv[s]]

    def b_copy(to, fro):
        return pltpu.make_async_remote_copy(
            src_ref=slots.at[pl.ds(SL * to, SL)],
            dst_ref=got.at[fro],
            send_sem=b_s,
            recv_sem=b_r,
            device_id=(d, to),
            device_id_type=MESH,
        )

    def b_all():
        ref = got.at[pl.ds(0, NPREC - 1)]
        return pltpu.make_async_remote_copy(
            src_ref=ref, dst_ref=ref, send_sem=b_s, recv_sem=b_r,
            device_id=(other, p), device_id_type=MESH,
        )

    def e_copy(s, to, fro):
        return pltpu.make_async_remote_copy(
            src_ref=outgo.at[s, to],
            dst_ref=back.at[SL * fro + s],
            send_sem=e_s.at[s],
            recv_sem=e_r.at[s],
            device_id=(d, to),
            device_id_type=MESH,
        )

    def e_all(s):
        ref = outgo.at[s, pl.ds(0, NPREC - 1)]
        return pltpu.make_async_remote_copy(
            src_ref=ref, dst_ref=ref, send_sem=e_s.at[s], recv_sem=e_r.at[s],
            device_id=(other, p), device_id_type=MESH,
        )

    def n_copy(s, to, fro):
        return pltpu.make_async_remote_copy(
            src_ref=norm.at[s],
            dst_ref=norms.at[s, fro],
            send_sem=n_s.at[s],
            recv_sem=n_r.at[s],
            device_id=(to, p),
            device_id_type=MESH,
        )

    def n_all(s):
        ref = norms.at[s, pl.ds(0, NDP - 1)]
        return pltpu.make_async_remote_copy(
            src_ref=ref, dst_ref=ref, send_sem=n_s.at[s], recv_sem=n_r.at[s],
            device_id=(other, p), device_id_type=MESH,
        )

    @pl.loop(1, NPREC)
    def _(i):
        b_copy((p + i) % NPREC, p).start()

    got[p] = slots[pl.ds(SL * p, SL)]

    for s in (1, 2):
        ring_step(wall, RR, RD, s, 1)
    for k in (2, 3):
        for s in range(SL):
            ring_step(wall, RR, RD, s, k)

    def own_strip(s):
        rows = got[:, s].astype(F32).reshape(NPREC * Q, LANES)
        strip_t[...] = rows
        square = jnp.sum(jnp.sum(rows * rows, axis=0, keepdims=True), axis=1, keepdims=True)
        norm[s] = jnp.broadcast_to(square, (8, LANES))
        for c in range(8):
            for r in range(2):
                strip_m[c, pl.ds(r, NPREC, stride=2), :] = strip_t[
                    pl.ds(2 * c + r, NPREC, stride=Q), :
                ]
        for c in range(8):
            gall[s, d, :, c * LANES : (c + 1) * LANES] = strip_m[c].astype(BF)

    def whole_root(s, a):
        for b in range(NY):
            w = (b - a) % NY
            if w < WIN:
                block = wall[s, 2 * a : 2 * a + 2, :, w * LANES : (w + 1) * LANES]
                block = block.reshape(LANES, LANES)
            else:
                w = NY - w
                block = wall[s, 2 * b : 2 * b + 2, :, w * LANES : (w + 1) * LANES]
                block = block.reshape(LANES, LANES).T
            rfull[s, a * LANES : (a + 1) * LANES, b * LANES : (b + 1) * LANES] = block

    def chips(k):
        return [wrap(y + k)] if k in (0, 4) else [wrap(y + k), wrap(y - k)]

    def chip_rows(s, k):
        return jnp.concatenate(
            [gall[s, pl.ds(2 * c, 2)].reshape(LANES, ORDER) for c in chips(k)], axis=0
        )

    def add_products(s, k):
        lhs = []
        for c in chips(k):
            here = pl.ds(pl.multiple_of(c * LANES, LANES), LANES)
            mine = pl.ds(pl.multiple_of(y * LANES, LANES), LANES)
            cols = gall[s, pl.ds(2 * c, 2), :, mine].reshape(LANES, LANES).T
            cols = jnp.where(core == 0, cols[:STRIP], cols[STRIP:])
            lhs.append(jnp.concatenate([lroot[s, :, here], cols], axis=0))
        lhs = jnp.concatenate(lhs, axis=1)
        rhs = chip_rows(s, k)
        for n in range(ORDER // TILE):
            tile = slice(n * TILE, (n + 1) * TILE)
            res = jnp.dot(lhs, rhs[:, tile], preferred_element_type=F32)
            if k == 0:
                half_acc[s, :, tile] = res[:STRIP]
                right_out[s, :, tile] = res[STRIP:]
            elif k < 4:
                half_acc[s, :, tile] += res[:STRIP]
                right_out[s, :, tile] += res[STRIP:]
            else:
                half[:, tile] = (half_acc[s, :, tile] + res[:STRIP]).astype(BF)
                right_out[s, :, tile] += res[STRIP:]

    def left_product(s, k):
        res = lax.dot_general(
            gall[s, d], chip_rows(s, k), (((1,), (1,)), ((), ())), preferred_element_type=F32
        )
        for j, c in enumerate(chips(k)):
            here = pl.ds(pl.multiple_of(c * LANES, LANES), LANES)
            left_out[s, :, here] = res[:, j * LANES : (j + 1) * LANES]

    def precondition(s):
        square = jnp.zeros((1, TILE), F32)
        for n in range(ORDER // TILE):
            tile = slice(n * TILE, (n + 1) * TILE)
            pre = jnp.dot(half[...], rfull[s, :, tile], preferred_element_type=F32)
            square += jnp.sum(pre * pre, axis=0, keepdims=True)
            for h in range(TILE // LANES):
                prec_m[n * (TILE // LANES) + h] = pre[:, h * LANES : (h + 1) * LANES]
        norm[s, 0:1, :] = jnp.broadcast_to(jnp.sum(square, axis=1, keepdims=True), (1, LANES))

        @pl.loop(1, NDP)
        def _(i):
            n_copy(s, (d + i) % NDP, d).start()

        norms[s, d] = norm[s]
        for c in range(8):
            for r in range(2):
                strip_t[pl.ds(2 * c + r, NPREC, stride=Q), :] = prec_m[
                    c, pl.ds(r, NPREC, stride=2), :
                ]

    def send_back(s):
        n_all(s).wait_recv()
        total = jnp.sum(norms[s], axis=0)
        factor = jnp.sqrt(total[1:2]) / (jnp.sqrt(total[0:1]) + 1e-06)
        outgo[s] = (strip_t[...] * factor).astype(BF).reshape(NPREC, Q, LANES)

        @pl.loop(1, NPREC)
        def _(i):
            e_copy(s, (p + i) % NPREC, p).start()

        back[SL * p + s] = outgo[s, p]

    def out_copies(s):
        return [
            pltpu.make_async_copy(left_out.at[s], left_hbm.at[s], out_sem.at[0, s]),
            pltpu.make_async_copy(right_out.at[s], right_hbm.at[s], out_sem.at[1, s]),
        ]

    def grams(s, k):
        ring_other(gall, GD, s, k)
        add_products(s, k)
        left_product(s, k)

    def step(s, k):
        ring_step(gall, GR, GD, s, k)

    def finish(s):
        ring_other(gall, GD, s, 4)
        add_products(s, 4)
        precondition(s)
        left_product(s, 4)
        for copy in out_copies(s):
            copy.start()

    b_all().wait_recv()
    own_strip(0)
    ring_start(gall, GR, GD, 0)
    own_strip(1)
    ring_start(gall, GR, GD, 1)
    for s in range(SL):
        ring_step(wall, RR, RD, s, 4)
    step(0, 1)
    own_strip(2)
    ring_start(gall, GR, GD, 2)
    grams(0, 0)
    step(1, 1)
    grams(1, 0)
    grams(0, 1)
    step(0, 2)
    grams(1, 1)
    step(2, 1)
    grams(0, 2)
    grams(2, 0)
    step(1, 2)
    for s in range(SL):
        for k in range(5):
            ring_other(wall, RD, s, k)
    for a in range(4):
        whole_root(0, a)
    step(0, 3)
    grams(2, 1)
    for a in range(4, NY):
        whole_root(0, a)
    step(2, 2)
    grams(1, 2)
    grams(0, 3)
    step(1, 3)
    grams(2, 2)
    for a in range(4):
        whole_root(1, a)
    step(0, 4)
    grams(1, 3)
    finish(0)
    step(2, 3)
    for a in range(4, NY):
        whole_root(1, a)
    send_back(0)
    step(1, 4)
    for a in range(4):
        whole_root(2, a)
    grams(2, 3)
    finish(1)
    step(2, 4)
    for a in range(4, NY):
        whole_root(2, a)
    send_back(1)
    finish(2)

    for s in range(SL):
        ring_drain(wall, RR, RD, s)
        ring_drain(gall, GR, GD, s)
        n_all(s).wait_send()
    for g in range(2):
        for t in range(NY):
            sib_part(g, t).wait_send()
            if t < NY - 1:
                for u in range(2):
                    rs_copy(g, t, u).wait_send()
    b_all().wait_send()
    for s in range(2):
        e_all(s).wait_send()
        e_all(s).wait_recv()
    send_back(2)
    e_all(2).wait_send()
    e_all(2).wait_recv()

    @pl.loop(0, NB, unroll=8)
    def _(b):
        upd_out[b] = back[table[b]]

    last = pltpu.make_async_copy(upd_out, upd_hbm, out_sem.at[2, 0])
    last.start()
    for s in range(SL):
        for copy in out_copies(s):
            copy.wait()
    last.wait()


def hand_over(left_in, right_in, upd_in, left, right, upd, sem):
    copies = [pltpu.make_async_copy(upd_in, upd, sem.at[2, 0])]
    for s in range(SL):
        copies.append(pltpu.make_async_copy(left_in.at[s], left.at[s], sem.at[0, s]))
        copies.append(pltpu.make_async_copy(right_in.at[s], right.at[s], sem.at[1, s]))
    for copy in copies:
        copy.start()
    for copy in copies:
        copy.wait()


def body(grad_part, table, left_root, right_root):
    grad = grad_part.reshape(NB, NDP, 2, 8, LANES).transpose(0, 1, 3, 2, 4)
    grad = grad.reshape(NB, NDP, Q, LANES)
    slot = jnp.arange(SL * NPREC, dtype=jnp.int32)
    block = jnp.arange(NB, dtype=jnp.int32) - NB
    named = slot[:, None] == table[None, :]
    inv = NB + jnp.sum(jnp.where(named, block[None, :], 0), axis=1, dtype=jnp.int32)
    vmem = pl.BlockSpec(memory_space=pltpu.VMEM)
    smem = pl.BlockSpec(memory_space=pltpu.SMEM)
    hbm = pl.BlockSpec(memory_space=pl.ANY)
    dma = pltpu.SemaphoreType.DMA
    results = [
        jax.ShapeDtypeStruct((SL, STRIP, ORDER), F32),
        jax.ShapeDtypeStruct((SL, STRIP, ORDER), F32),
        jax.ShapeDtypeStruct((NB, Q, LANES), BF),
    ]
    out = pl.pallas_call(
        kernel,
        out_shape=results,
        in_specs=[smem, smem, hbm, vmem, vmem],
        out_specs=[hbm, hbm, hbm],
        scratch_shapes=[
            pltpu.VMEM((NY, NB, Q, LANES), BF),
            pltpu.VMEM((NY, NB, Q, LANES), BF),
            pltpu.VMEM((2, NY - 1, HALF, Q, LANES), BF),
            pltpu.VMEM((NB + 1, Q, LANES), BF),
            pltpu.VMEM((SL * NPREC, Q, LANES), BF),
            pltpu.VMEM((NPREC, SL, Q, LANES), BF),
            pltpu.VMEM((NPREC * Q, LANES), F32),
            pltpu.VMEM((8, STRIP, LANES), F32),
            pltpu.VMEM((SL, NDP, STRIP, ORDER), BF),
            pltpu.VMEM((SL, NDP, STRIP, WIN * LANES), BF),
            pltpu.VMEM((SL, ORDER, ORDER), BF),
            pltpu.VMEM((SL, STRIP, ORDER), F32),
            pltpu.VMEM((STRIP, ORDER), BF),
            pltpu.VMEM((8, STRIP, LANES), F32),
            pltpu.VMEM((SL, NPREC, Q, LANES), BF),
            pltpu.VMEM((SL * NPREC, Q, LANES), BF),
            pltpu.VMEM((SL, 8, LANES), F32),
            pltpu.VMEM((SL, NDP, 8, LANES), F32),
            pltpu.VMEM((SL, STRIP, ORDER), F32),
            pltpu.VMEM((SL, STRIP, ORDER), F32),
            pltpu.VMEM((NB, Q, LANES), BF),
            dma((2, NY)), dma((2, NY)), dma((2, NY)),
            dma((2, NY - 1, 2)), dma((2, NY - 1, 2)),
            dma, dma,
            dma((SL, 2, 4)), dma((SL, 2, 4)), dma((SL, 9)), dma((SL, 9)),
            dma((SL, 2, 4)), dma((SL, 2, 4)), dma((SL, 9)), dma((SL, 9)),
            dma((SL,)), dma((SL,)),
            dma((SL,)), dma((SL,)),
            dma((3, SL)),
        ],
        compiler_params=pltpu.CompilerParams(
            collective_id=0, has_side_effects=True, vmem_limit_bytes=56 * 2**20
        ),
        cost_estimate=pl.CostEstimate(
            flops=2 * SL * 5 * STRIP * ORDER * ORDER, bytes_accessed=8 * 2**20, transcendentals=0
        ),
        name="shampoo_step",
    )(inv, table, grad, left_root, right_root)
    left, right, upd = pl.pallas_call(
        hand_over,
        out_shape=results,
        in_specs=[hbm, hbm, hbm],
        out_specs=[hbm, hbm, hbm],
        scratch_shapes=[dma((3, SL))],
        compiler_params=pltpu.CompilerParams(vmem_limit_bytes=56 * 2**20),
        name="hand_over",
    )(*out)
    update = upd.reshape(NB, 8, 2, LANES).transpose(0, 2, 1, 3).reshape(NB, 1, 1, 2, ORDER)
    return (left, right, update)


def solution(mesh):
    in_specs = (
        P("dp", None, None, "prec", None, None),
        P(),
        P("prec", "dp", None),
        P("prec", "dp", None),
    )
    out_specs = (P("prec", "dp", None), P("prec", "dp", None), P(None, "dp", "prec", None, None))
    return jax.shard_map(body, mesh=mesh, in_specs=in_specs, out_specs=out_specs, check_vma=False)
```

```python
import jax
import jax.numpy as jnp
from jax import lax
from jax.experimental import pallas as pl
from jax.experimental.pallas import tpu as pltpu
from jax.sharding import PartitionSpec as P

MESH = pl.DeviceIdType.MESH
BF = jnp.bfloat16
F32 = jnp.float32

NY = 8
NDP = 16
NPREC = 32
SL = 3
NB = 40
STRIP = 64
ORDER = 1024
LANES = 128
Q = 16
HALF = NB // 2
WIN = 5
TILE = 256
SIGNS = (1, -1)


def kernel(
    inv, table, grad, lroot, rroot, left_hbm, right_hbm, upd_hbm,
    part, sib, ringbuf, summed, slots, got, strip_t, strip_m, gall, wall, rfull,
    half_acc, half, prec_m, outgo, back, norm, norms, left_out, right_out, upd_out,
    part_sem, sib_s, sib_r, rs_s, rs_r, b_s, b_r,
    rr_s, rr_r, rd_s, rd_r, gr_s, gr_r, gd_s, gd_r,
    e_s, e_r, n_s, n_r, out_sem,
):
    d = lax.axis_index("dp")
    p = lax.axis_index("prec")
    y = d // 2
    core = d % 2
    other = 2 * y + (1 - core)

    def wrap(v):
        return (v + 4 * NY) % NY

    def dp_of(chip_y):
        return 2 * chip_y + core

    barrier = pltpu.get_barrier_semaphore()

    @pl.loop(1, NDP)
    def _(i):
        pl.semaphore_signal(barrier, inc=1, device_id=((d + i) % NDP, p), device_id_type=MESH)

    @pl.loop(1, NPREC)
    def _(i):
        pl.semaphore_signal(barrier, inc=1, device_id=(d, (p + i) % NPREC), device_id_type=MESH)

    def chunk(g, t):
        return wrap(y + SIGNS[g] * (4 - t))

    def share(g, t):
        return pl.ds(g * HALF, HALF) if t in (0, 4) else pl.ds(0, NB)

    def local_part(g, t):
        c = chunk(g, t)
        return pltpu.make_async_copy(
            grad.at[share(g, t), 2 * c + core], part.at[c, share(g, t)], part_sem.at[g, t]
        )

    def sib_part(g, t):
        c = chunk(g, t)
        return pltpu.make_async_remote_copy(
            src_ref=grad.at[share(g, t), 2 * c + (1 - core)],
            dst_ref=sib.at[c, share(g, t)],
            send_sem=sib_s.at[g, t],
            recv_sem=sib_r.at[g, t],
            device_id=(other, p),
            device_id_type=MESH,
        )

    for t in range(5):
        for g in range(2):
            local_part(g, t).start()

    for w in range(WIN):
        cols = pl.ds(pl.multiple_of(wrap(y + w) * LANES, LANES), LANES)
        for s in range(SL):
            wall[s, d, :, w * LANES : (w + 1) * LANES] = rroot[s, :, cols]

    pl.semaphore_wait(barrier, NDP + NPREC - 2)
    for t in range(5):
        for g in range(2):
            sib_part(g, t).start()

    def hop(buf, ss, rs, s, g, k):
        o = wrap(y - SIGNS[g] * (k - 1))
        rows = pl.ds(0, STRIP) if k < 4 else pl.ds(g * (STRIP // 2), STRIP // 2)
        ref = buf.at[s, dp_of(o), rows]
        return pltpu.make_async_remote_copy(
            src_ref=ref,
            dst_ref=ref,
            send_sem=ss.at[s, g, k - 1],
            recv_sem=rs.at[s, g, k - 1],
            device_id=(dp_of(wrap(y + SIGNS[g])), p),
            device_id_type=MESH,
        )

    def landing(buf, ss, rs, s, g, k):
        o = wrap(y - SIGNS[g] * k)
        rows = pl.ds(0, STRIP) if k < 4 else pl.ds(g * (STRIP // 2), STRIP // 2)
        ref = buf.at[s, dp_of(o), rows]
        return pltpu.make_async_remote_copy(
            src_ref=ref,
            dst_ref=ref,
            send_sem=ss.at[s, g, k - 1],
            recv_sem=rs.at[s, g, k - 1],
            device_id=(dp_of(wrap(y + SIGNS[g])), p),
            device_id_type=MESH,
        )

    def across(buf, ss, rs, s, g, k, mine):
        o = wrap(y - SIGNS[g] * k)
        rows = pl.ds(0, STRIP) if k < 4 else pl.ds(g * (STRIP // 2), STRIP // 2)
        ref = buf.at[s, 2 * o + (core if mine else 1 - core), rows]
        n = 0 if k == 0 else 1 + g * 4 + (k - 1)
        return pltpu.make_async_remote_copy(
            src_ref=ref,
            dst_ref=ref,
            send_sem=ss.at[s, n],
            recv_sem=rs.at[s, n],
            device_id=(other, p),
            device_id_type=MESH,
        )

    def ring_start(buf, rsem, dsem, s):
        for g in range(2):
            hop(buf, *rsem, s, g, 1).start()
        across(buf, *dsem, s, 0, 0, True).start()

    def ring_step(buf, rsem, dsem, s, k):
        for g in range(2):
            landing(buf, *rsem, s, g, k).wait_recv()
            if k < 4:
                hop(buf, *rsem, s, g, k + 1).start()
            across(buf, *dsem, s, g, k, True).start()

    def ring_other(buf, dsem, s, k):
        for g in range(2 if k else 1):
            across(buf, *dsem, s, g, k, False).wait_recv()

    def ring_drain(buf, rsem, dsem, s):
        for k in range(5):
            for g in range(2 if k else 1):
                if k:
                    hop(buf, *rsem, s, g, k).wait_send()
                across(buf, *dsem, s, g, k, True).wait_send()

    RR, RD, GR, GD = (rr_s, rr_r), (rd_s, rd_r), (gr_s, gr_r), (gd_s, gd_r)

    def rs_copy(g, t, h):
        return pltpu.make_async_remote_copy(
            src_ref=part.at[chunk(g, t), pl.ds(h * HALF, HALF)],
            dst_ref=ringbuf.at[g, t, pl.ds(h * HALF, HALF)],
            send_sem=rs_s.at[g, t, h],
            recv_sem=rs_r.at[g, t, h],
            device_id=(dp_of(wrap(y + SIGNS[g])), p),
            device_id_type=MESH,
        )

    def rs_step(g, t, h):
        blocks = pl.ds(h * HALF, HALF)
        c = chunk(g, t)
        total = part[c, blocks].astype(F32) + sib[c, blocks].astype(F32)
        if t > 1 or (t == 1 and h == g):
            rs_copy(g, t - 1, h).wait_recv()
            total += ringbuf[g, t - 1, blocks].astype(F32)
        part[c, blocks] = total.astype(BF)
        rs_copy(g, t, h).start()

    def rs_ready(t):
        for g in range(2):
            local_part(g, t).wait()
            sib_part(g, t).wait_recv()

    ring_start(wall, RR, RD, 0)
    rs_ready(0)
    for g in range(2):
        rs_step(g, 0, g)
    for t in range(1, 4):
        rs_ready(t)
        for g in range(2):
            rs_step(g, t, 1 - g)
        for g in range(2):
            rs_step(g, t, g)
    ring_start(wall, RR, RD, 1)
    for h in range(2):
        local_part(h, 4).wait()
        sib_part(h, 4).wait_recv()
        blocks = pl.ds(h * HALF, HALF)
        total = part[y, blocks].astype(F32) + sib[y, blocks].astype(F32)
        for g in range(2):
            rs_copy(g, 3, h).wait_recv()
            total += ringbuf[g, 3, blocks].astype(F32)
        summed[pl.ds(1 + h * HALF, HALF)] = total.astype(BF)
    summed[0] = jnp.zeros((Q, LANES), BF)

    @pl.loop(0, SL * NPREC, unroll=8)
    def _(s):
        slots[s] = summed[inv[s]]

    def b_copy(to, fro):
        return pltpu.make_async_remote_copy(
            src_ref=slots.at[pl.ds(SL * to, SL)],
            dst_ref=got.at[fro],
            send_sem=b_s,
            recv_sem=b_r,
            device_id=(d, to),
            device_id_type=MESH,
        )

    def b_all():
        ref = got.at[pl.ds(0, NPREC - 1)]
        return pltpu.make_async_remote_copy(
            src_ref=ref, dst_ref=ref, send_sem=b_s, recv_sem=b_r,
            device_id=(other, p), device_id_type=MESH,
        )

    def e_copy(s, to, fro):
        return pltpu.make_async_remote_copy(
            src_ref=outgo.at[s, to],
            dst_ref=back.at[SL * fro + s],
            send_sem=e_s.at[s],
            recv_sem=e_r.at[s],
            device_id=(d, to),
            device_id_type=MESH,
        )

    def e_all(s):
        ref = outgo.at[s, pl.ds(0, NPREC - 1)]
        return pltpu.make_async_remote_copy(
            src_ref=ref, dst_ref=ref, send_sem=e_s.at[s], recv_sem=e_r.at[s],
            device_id=(other, p), device_id_type=MESH,
        )

    def n_copy(s, to, fro):
        return pltpu.make_async_remote_copy(
            src_ref=norm.at[s],
            dst_ref=norms.at[s, fro],
            send_sem=n_s.at[s],
            recv_sem=n_r.at[s],
            device_id=(to, p),
            device_id_type=MESH,
        )

    def n_all(s):
        ref = norms.at[s, pl.ds(0, NDP - 1)]
        return pltpu.make_async_remote_copy(
            src_ref=ref, dst_ref=ref, send_sem=n_s.at[s], recv_sem=n_r.at[s],
            device_id=(other, p), device_id_type=MESH,
        )

    @pl.loop(1, NPREC)
    def _(i):
        b_copy((p + i) % NPREC, p).start()

    got[p] = slots[pl.ds(SL * p, SL)]

    ring_start(wall, RR, RD, 2)

    def own_strip(s):
        rows = got[:, s].astype(F32).reshape(NPREC * Q, LANES)
        strip_t[...] = rows
        square = jnp.sum(jnp.sum(rows * rows, axis=0, keepdims=True), axis=1, keepdims=True)
        norm[s] = jnp.broadcast_to(square, (8, LANES))
        for c in range(8):
            for r in range(2):
                strip_m[c, pl.ds(r, NPREC, stride=2), :] = strip_t[
                    pl.ds(2 * c + r, NPREC, stride=Q), :
                ]
        for c in range(8):
            gall[s, d, :, c * LANES : (c + 1) * LANES] = strip_m[c].astype(BF)

    def whole_root(s, k):
        ring_other(wall, RD, s, k)
        for a in sorted({k, (NY - k) % NY}):
            strip = wall[s, pl.ds(2 * wrap(y + a), 2)].reshape(LANES, WIN * LANES)
            for w in range(WIN):
                b = (a + w) % NY
                block = strip[:, w * LANES : (w + 1) * LANES]
                rfull[s, a * LANES : (a + 1) * LANES, b * LANES : (b + 1) * LANES] = block
                if 0 < w < WIN - 1:
                    rfull[s, b * LANES : (b + 1) * LANES, a * LANES : (a + 1) * LANES] = block.T

    def chips(k):
        return [wrap(y + k)] if k in (0, 4) else [wrap(y + k), wrap(y - k)]

    def chip_rows(s, k):
        return jnp.concatenate(
            [gall[s, pl.ds(2 * c, 2)].reshape(LANES, ORDER) for c in chips(k)], axis=0
        )

    def add_products(s, k):
        lhs = []
        for c in chips(k):
            here = pl.ds(pl.multiple_of(c * LANES, LANES), LANES)
            mine = pl.ds(pl.multiple_of(y * LANES, LANES), LANES)
            cols = gall[s, pl.ds(2 * c, 2), :, mine].reshape(LANES, LANES).T
            cols = jnp.where(core == 0, cols[:STRIP], cols[STRIP:])
            lhs.append(jnp.concatenate([lroot[s, :, here], cols], axis=0))
        lhs = jnp.concatenate(lhs, axis=1)
        rhs = chip_rows(s, k)
        for n in range(ORDER // TILE):
            tile = slice(n * TILE, (n + 1) * TILE)
            res = jnp.dot(lhs, rhs[:, tile], preferred_element_type=F32)
            if k == 0:
                half_acc[s, :, tile] = res[:STRIP]
                right_out[s, :, tile] = res[STRIP:]
            elif k < 4:
                half_acc[s, :, tile] += res[:STRIP]
                right_out[s, :, tile] += res[STRIP:]
            else:
                half[:, tile] = (half_acc[s, :, tile] + res[:STRIP]).astype(BF)
                right_out[s, :, tile] += res[STRIP:]

    def left_product(s, k):
        res = lax.dot_general(
            gall[s, d], chip_rows(s, k), (((1,), (1,)), ((), ())), preferred_element_type=F32
        )
        for j, c in enumerate(chips(k)):
            here = pl.ds(pl.multiple_of(c * LANES, LANES), LANES)
            left_out[s, :, here] = res[:, j * LANES : (j + 1) * LANES]

    def precondition(s):
        square = jnp.zeros((1, TILE), F32)
        near = [wrap(y + a) for a in range(NY)]
        lhs = jnp.concatenate(
            [half[:, pl.ds(pl.multiple_of(c * LANES, LANES), LANES)] for c in near], axis=1
        )
        for n in range(ORDER // TILE):
            tile = slice(n * TILE, (n + 1) * TILE)
            pre = jnp.dot(lhs, rfull[s, :, tile], preferred_element_type=F32)
            square += jnp.sum(pre * pre, axis=0, keepdims=True)
            for h in range(TILE // LANES):
                prec_m[near[n * (TILE // LANES) + h]] = pre[:, h * LANES : (h + 1) * LANES]
        norm[s, 0:1, :] = jnp.broadcast_to(jnp.sum(square, axis=1, keepdims=True), (1, LANES))

        @pl.loop(1, NDP)
        def _(i):
            n_copy(s, (d + i) % NDP, d).start()

        norms[s, d] = norm[s]
        for c in range(8):
            for r in range(2):
                strip_t[pl.ds(2 * c + r, NPREC, stride=Q), :] = prec_m[
                    c, pl.ds(r, NPREC, stride=2), :
                ]

    def send_back(s):
        n_all(s).wait_recv()
        total = jnp.sum(norms[s], axis=0)
        factor = jnp.sqrt(total[1:2]) / (jnp.sqrt(total[0:1]) + 1e-06)
        outgo[s] = (strip_t[...] * factor).astype(BF).reshape(NPREC, Q, LANES)

        @pl.loop(1, NPREC)
        def _(i):
            e_copy(s, (p + i) % NPREC, p).start()

        back[SL * p + s] = outgo[s, p]

    def out_copies(s):
        return [
            pltpu.make_async_copy(left_out.at[s], left_hbm.at[s], out_sem.at[0, s]),
            pltpu.make_async_copy(right_out.at[s], right_hbm.at[s], out_sem.at[1, s]),
        ]

    def grams(s, k):
        ring_other(gall, GD, s, k)
        add_products(s, k)
        left_product(s, k)

    def step(s, k):
        ring_step(gall, GR, GD, s, k)

    def finish(s):
        ring_other(gall, GD, s, 4)
        add_products(s, 4)
        precondition(s)
        left_product(s, 4)
        for copy in out_copies(s):
            copy.start()

    for s in range(SL):
        ring_step(wall, RR, RD, s, 1)
        whole_root(s, 0)
    for s in range(SL):
        ring_step(wall, RR, RD, s, 2)
        whole_root(s, 1)
    ring_step(wall, RR, RD, 0, 3)
    whole_root(0, 2)
    b_all().wait_recv()
    own_strip(0)
    ring_start(gall, GR, GD, 0)
    ring_step(wall, RR, RD, 1, 3)
    ring_step(wall, RR, RD, 2, 3)
    own_strip(1)
    ring_start(gall, GR, GD, 1)
    whole_root(1, 2)
    own_strip(2)
    whole_root(2, 2)
    grams(0, 0)
    step(0, 1)
    ring_start(gall, GR, GD, 2)
    whole_root(0, 3)
    grams(1, 0)
    step(1, 1)
    whole_root(1, 3)
    grams(0, 1)
    step(0, 2)
    for s in range(SL):
        ring_step(wall, RR, RD, s, 4)
    whole_root(2, 3)
    grams(1, 1)
    step(2, 1)
    grams(0, 2)
    grams(2, 0)
    step(1, 2)
    whole_root(0, 4)
    grams(2, 1)
    step(0, 3)
    grams(1, 2)
    step(2, 2)
    grams(0, 3)
    whole_root(1, 4)
    step(1, 3)
    grams(2, 2)
    step(0, 4)
    grams(1, 3)
    step(2, 3)
    finish(0)
    step(1, 4)
    grams(2, 3)
    send_back(0)
    finish(1)
    step(2, 4)
    whole_root(2, 4)
    send_back(1)
    finish(2)

    for s in range(SL):
        ring_drain(wall, RR, RD, s)
        ring_drain(gall, GR, GD, s)
        n_all(s).wait_send()
    for g in range(2):
        for t in range(5):
            sib_part(g, t).wait_send()
        for t in range(4):
            for h in range(2):
                if t or h == g:
                    rs_copy(g, t, h).wait_send()
    b_all().wait_send()
    for s in range(2):
        e_all(s).wait_send()
        e_all(s).wait_recv()
    send_back(2)
    e_all(2).wait_send()
    e_all(2).wait_recv()

    @pl.loop(0, NB, unroll=8)
    def _(b):
        upd_out[b] = back[table[b]]

    last = pltpu.make_async_copy(upd_out, upd_hbm, out_sem.at[2, 0])
    last.start()
    for s in range(SL):
        for copy in out_copies(s):
            copy.wait()
    last.wait()


def hand_over(left_in, right_in, upd_in, left, right, upd, sem):
    copies = [pltpu.make_async_copy(upd_in, upd, sem.at[2, 0])]
    for s in range(SL):
        copies.append(pltpu.make_async_copy(left_in.at[s], left.at[s], sem.at[0, s]))
        copies.append(pltpu.make_async_copy(right_in.at[s], right.at[s], sem.at[1, s]))
    for copy in copies:
        copy.start()
    for copy in copies:
        copy.wait()


def body(grad_part, table, left_root, right_root):
    grad = grad_part.reshape(NB, NDP, 2, 8, LANES).transpose(0, 1, 3, 2, 4)
    grad = grad.reshape(NB, NDP, Q, LANES)
    slot = jnp.arange(SL * NPREC, dtype=jnp.int32)
    block = jnp.arange(1, NB + 1, dtype=jnp.int32)
    named = slot[:, None] == table[None, :]
    inv = jnp.sum(jnp.where(named, block[None, :], 0), axis=1, dtype=jnp.int32)
    vmem = pl.BlockSpec(memory_space=pltpu.VMEM)
    smem = pl.BlockSpec(memory_space=pltpu.SMEM)
    hbm = pl.BlockSpec(memory_space=pl.ANY)
    dma = pltpu.SemaphoreType.DMA
    results = [
        jax.ShapeDtypeStruct((SL, STRIP, ORDER), F32),
        jax.ShapeDtypeStruct((SL, STRIP, ORDER), F32),
        jax.ShapeDtypeStruct((NB, Q, LANES), BF),
    ]
    out = pl.pallas_call(
        kernel,
        out_shape=results,
        in_specs=[smem, smem, hbm, vmem, vmem],
        out_specs=[hbm, hbm, hbm],
        scratch_shapes=[
            pltpu.VMEM((NY, NB, Q, LANES), BF),
            pltpu.VMEM((NY, NB, Q, LANES), BF),
            pltpu.VMEM((2, 4, NB, Q, LANES), BF),
            pltpu.VMEM((NB + 1, Q, LANES), BF),
            pltpu.VMEM((SL * NPREC, Q, LANES), BF),
            pltpu.VMEM((NPREC, SL, Q, LANES), BF),
            pltpu.VMEM((NPREC * Q, LANES), F32),
            pltpu.VMEM((8, STRIP, LANES), F32),
            pltpu.VMEM((SL, NDP, STRIP, ORDER), BF),
            pltpu.VMEM((SL, NDP, STRIP, WIN * LANES), BF),
            pltpu.VMEM((SL, ORDER, ORDER), BF),
            pltpu.VMEM((SL, STRIP, ORDER), F32),
            pltpu.VMEM((STRIP, ORDER), BF),
            pltpu.VMEM((8, STRIP, LANES), F32),
            pltpu.VMEM((SL, NPREC, Q, LANES), BF),
            pltpu.VMEM((SL * NPREC, Q, LANES), BF),
            pltpu.VMEM((SL, 8, LANES), F32),
            pltpu.VMEM((SL, NDP, 8, LANES), F32),
            pltpu.VMEM((SL, STRIP, ORDER), F32),
            pltpu.VMEM((SL, STRIP, ORDER), F32),
            pltpu.VMEM((NB, Q, LANES), BF),
            dma((2, 5)), dma((2, 5)), dma((2, 5)),
            dma((2, 4, 2)), dma((2, 4, 2)),
            dma, dma,
            dma((SL, 2, 4)), dma((SL, 2, 4)), dma((SL, 9)), dma((SL, 9)),
            dma((SL, 2, 4)), dma((SL, 2, 4)), dma((SL, 9)), dma((SL, 9)),
            dma((SL,)), dma((SL,)),
            dma((SL,)), dma((SL,)),
            dma((3, SL)),
        ],
        compiler_params=pltpu.CompilerParams(
            collective_id=0, has_side_effects=True, vmem_limit_bytes=56 * 2**20
        ),
        cost_estimate=pl.CostEstimate(
            flops=2 * SL * 5 * STRIP * ORDER * ORDER, bytes_accessed=8 * 2**20, transcendentals=0
        ),
        name="shampoo_step",
    )(inv, table, grad, left_root, right_root)
    left, right, upd = pl.pallas_call(
        hand_over,
        out_shape=results,
        in_specs=[vmem, vmem, vmem],
        out_specs=[hbm, hbm, hbm],
        scratch_shapes=[dma((3, SL))],
        compiler_params=pltpu.CompilerParams(vmem_limit_bytes=56 * 2**20),
        name="hand_over",
    )(*out)
    update = upd.reshape(NB, 8, 2, LANES).transpose(0, 2, 1, 3).reshape(NB, 1, 1, 2, ORDER)
    return (left, right, update)


def solution(mesh):
    in_specs = (
        P("dp", None, None, "prec", None, None),
        P(),
        P("prec", "dp", None),
        P("prec", "dp", None),
    )
    out_specs = (P("prec", "dp", None), P("prec", "dp", None), P(None, "dp", "prec", None, None))
    return jax.shard_map(body, mesh=mesh, in_specs=in_specs, out_specs=out_specs, check_vma=False)
```

```python
import jax
import jax.numpy as jnp
from jax import lax
from jax.experimental import pallas as pl
from jax.experimental.pallas import tpu as pltpu
from jax.sharding import PartitionSpec as P

MESH = pl.DeviceIdType.MESH
BF = jnp.bfloat16
F32 = jnp.float32

NY = 8
NDP = 16
NPREC = 32
SL = 3
NB = 40
STRIP = 64
ORDER = 1024
LANES = 128
Q = 16
HALF = NB // 2
WIN = 5
TILE = 256
SIGNS = (1, -1)


def kernel(
    inv, table, grad, lroot, rroot, left_hbm, right_hbm, upd_hbm,
    part, sib, ringbuf, summed, slots, got, strip_t, strip_m, gall, wall, rfull,
    half_acc, half, prec_m, outgo, back, norm, norms, fac, facs, left_out, right_out, upd_out,
    part_sem, sib_s, sib_r, rs_s, rs_r, b_s, b_r,
    rr_s, rr_r, rd_s, rd_r, gr_s, gr_r, gd_s, gd_r,
    e_s, e_r, n_s, n_r, f_s, f_r, out_sem,
):
    d = lax.axis_index("dp")
    p = lax.axis_index("prec")
    y = d // 2
    core = d % 2
    other = 2 * y + (1 - core)

    def wrap(v):
        return (v + 4 * NY) % NY

    def dp_of(chip_y):
        return 2 * chip_y + core

    barrier = pltpu.get_barrier_semaphore()

    @pl.loop(1, NDP)
    def _(i):
        pl.semaphore_signal(barrier, inc=1, device_id=((d + i) % NDP, p), device_id_type=MESH)

    @pl.loop(1, NPREC)
    def _(i):
        pl.semaphore_signal(barrier, inc=1, device_id=(d, (p + i) % NPREC), device_id_type=MESH)

    def chunk(g, t):
        return wrap(y + SIGNS[g] * (4 - t))

    def share(g, t):
        return pl.ds(g * HALF, HALF) if t in (0, 4) else pl.ds(0, NB)

    def local_part(g, t):
        c = chunk(g, t)
        return pltpu.make_async_copy(
            grad.at[share(g, t), 2 * c + core], part.at[c, share(g, t)], part_sem.at[g, t]
        )

    def sib_part(g, t):
        c = chunk(g, t)
        return pltpu.make_async_remote_copy(
            src_ref=grad.at[share(g, t), 2 * c + (1 - core)],
            dst_ref=sib.at[c, share(g, t)],
            send_sem=sib_s.at[g, t],
            recv_sem=sib_r.at[g, t],
            device_id=(other, p),
            device_id_type=MESH,
        )

    for t in range(5):
        for g in range(2):
            local_part(g, t).start()

    for w in range(WIN):
        cols = pl.ds(pl.multiple_of(wrap(y + w) * LANES, LANES), LANES)
        for s in range(SL):
            wall[s, d, :, w * LANES : (w + 1) * LANES] = rroot[s, :, cols]

    pl.semaphore_wait(barrier, NDP + NPREC - 2)
    for t in range(5):
        for g in range(2):
            sib_part(g, t).start()

    def hop(buf, ss, rs, s, g, k):
        o = wrap(y - SIGNS[g] * (k - 1))
        rows = pl.ds(0, STRIP) if k < 4 else pl.ds(g * (STRIP // 2), STRIP // 2)
        ref = buf.at[s, dp_of(o), rows]
        return pltpu.make_async_remote_copy(
            src_ref=ref,
            dst_ref=ref,
            send_sem=ss.at[s, g, k - 1],
            recv_sem=rs.at[s, g, k - 1],
            device_id=(dp_of(wrap(y + SIGNS[g])), p),
            device_id_type=MESH,
        )

    def landing(buf, ss, rs, s, g, k):
        o = wrap(y - SIGNS[g] * k)
        rows = pl.ds(0, STRIP) if k < 4 else pl.ds(g * (STRIP // 2), STRIP // 2)
        ref = buf.at[s, dp_of(o), rows]
        return pltpu.make_async_remote_copy(
            src_ref=ref,
            dst_ref=ref,
            send_sem=ss.at[s, g, k - 1],
            recv_sem=rs.at[s, g, k - 1],
            device_id=(dp_of(wrap(y + SIGNS[g])), p),
            device_id_type=MESH,
        )

    def across(buf, ss, rs, s, g, k, mine):
        o = wrap(y - SIGNS[g] * k)
        rows = pl.ds(0, STRIP) if k < 4 else pl.ds(g * (STRIP // 2), STRIP // 2)
        ref = buf.at[s, 2 * o + (core if mine else 1 - core), rows]
        n = 0 if k == 0 else 1 + g * 4 + (k - 1)
        return pltpu.make_async_remote_copy(
            src_ref=ref,
            dst_ref=ref,
            send_sem=ss.at[s, n],
            recv_sem=rs.at[s, n],
            device_id=(other, p),
            device_id_type=MESH,
        )

    def ring_start(buf, rsem, dsem, s):
        for g in range(2):
            hop(buf, *rsem, s, g, 1).start()
        across(buf, *dsem, s, 0, 0, True).start()

    def ring_step(buf, rsem, dsem, s, k):
        for g in range(2):
            landing(buf, *rsem, s, g, k).wait_recv()
            if k < 4:
                hop(buf, *rsem, s, g, k + 1).start()
            across(buf, *dsem, s, g, k, True).start()

    def ring_other(buf, dsem, s, k):
        for g in range(2 if k else 1):
            across(buf, *dsem, s, g, k, False).wait_recv()

    def ring_drain(buf, rsem, dsem, s):
        for k in range(5):
            for g in range(2 if k else 1):
                if k:
                    hop(buf, *rsem, s, g, k).wait_send()
                across(buf, *dsem, s, g, k, True).wait_send()

    RR, RD, GR, GD = (rr_s, rr_r), (rd_s, rd_r), (gr_s, gr_r), (gd_s, gd_r)

    def rs_copy(g, t, h):
        return pltpu.make_async_remote_copy(
            src_ref=part.at[chunk(g, t), pl.ds(h * HALF, HALF)],
            dst_ref=ringbuf.at[g, t, pl.ds(h * HALF, HALF)],
            send_sem=rs_s.at[g, t, h],
            recv_sem=rs_r.at[g, t, h],
            device_id=(dp_of(wrap(y + SIGNS[g])), p),
            device_id_type=MESH,
        )

    def rs_step(g, t, h):
        blocks = pl.ds(h * HALF, HALF)
        c = chunk(g, t)
        total = part[c, blocks].astype(F32) + sib[c, blocks].astype(F32)
        if t > 1 or (t == 1 and h == g):
            rs_copy(g, t - 1, h).wait_recv()
            total += ringbuf[g, t - 1, blocks].astype(F32)
        part[c, blocks] = total.astype(BF)
        rs_copy(g, t, h).start()

    def rs_ready(t):
        for g in range(2):
            local_part(g, t).wait()
            sib_part(g, t).wait_recv()

    ring_start(wall, RR, RD, 0)
    rs_ready(0)
    for g in range(2):
        rs_step(g, 0, g)
    for t in range(1, 4):
        rs_ready(t)
        for g in range(2):
            rs_step(g, t, 1 - g)
        for g in range(2):
            rs_step(g, t, g)
    ring_start(wall, RR, RD, 1)
    for h in range(2):
        local_part(h, 4).wait()
        sib_part(h, 4).wait_recv()
        blocks = pl.ds(h * HALF, HALF)
        total = part[y, blocks].astype(F32) + sib[y, blocks].astype(F32)
        for g in range(2):
            rs_copy(g, 3, h).wait_recv()
            total += ringbuf[g, 3, blocks].astype(F32)
        summed[pl.ds(1 + h * HALF, HALF)] = total.astype(BF)
    summed[0] = jnp.zeros((Q, LANES), BF)

    @pl.loop(0, SL * NPREC, unroll=8)
    def _(s):
        slots[s] = summed[inv[s]]

    def b_copy(to, fro):
        return pltpu.make_async_remote_copy(
            src_ref=slots.at[pl.ds(SL * to, SL)],
            dst_ref=got.at[fro],
            send_sem=b_s,
            recv_sem=b_r,
            device_id=(d, to),
            device_id_type=MESH,
        )

    def b_all():
        ref = got.at[pl.ds(0, NPREC - 1)]
        return pltpu.make_async_remote_copy(
            src_ref=ref, dst_ref=ref, send_sem=b_s, recv_sem=b_r,
            device_id=(other, p), device_id_type=MESH,
        )

    def e_copy(s, to, fro):
        return pltpu.make_async_remote_copy(
            src_ref=outgo.at[s, to],
            dst_ref=back.at[SL * fro + s],
            send_sem=e_s.at[s],
            recv_sem=e_r.at[s],
            device_id=(d, to),
            device_id_type=MESH,
        )

    def e_all(s):
        ref = outgo.at[s, pl.ds(0, NPREC - 1)]
        return pltpu.make_async_remote_copy(
            src_ref=ref, dst_ref=ref, send_sem=e_s.at[s], recv_sem=e_r.at[s],
            device_id=(other, p), device_id_type=MESH,
        )

    def n_copy(s, to, fro):
        return pltpu.make_async_remote_copy(
            src_ref=norm.at[s],
            dst_ref=norms.at[s, fro],
            send_sem=n_s.at[s],
            recv_sem=n_r.at[s],
            device_id=(to, p),
            device_id_type=MESH,
        )

    def n_all(s):
        ref = norms.at[s, pl.ds(0, NDP - 1)]
        return pltpu.make_async_remote_copy(
            src_ref=ref, dst_ref=ref, send_sem=n_s.at[s], recv_sem=n_r.at[s],
            device_id=(other, p), device_id_type=MESH,
        )

    @pl.loop(1, NPREC)
    def _(i):
        b_copy((p + i) % NPREC, p).start()

    got[p] = slots[pl.ds(SL * p, SL)]

    ring_start(wall, RR, RD, 2)

    def own_strip(s):
        rows = got[:, s].astype(F32).reshape(NPREC * Q, LANES)
        strip_t[s] = rows
        square = jnp.sum(jnp.sum(rows * rows, axis=0, keepdims=True), axis=1, keepdims=True)
        norm[s] = jnp.broadcast_to(square, (8, LANES))
        for c in range(8):
            for r in range(2):
                strip_m[c, pl.ds(r, NPREC, stride=2), :] = strip_t[
                    s, pl.ds(2 * c + r, NPREC, stride=Q), :
                ]
        for c in range(8):
            gall[s, d, :, c * LANES : (c + 1) * LANES] = strip_m[c].astype(BF)

    def whole_root(s, k):
        ring_other(wall, RD, s, k)
        for a in sorted({k, (NY - k) % NY}):
            strip = wall[s, pl.ds(2 * wrap(y + a), 2)].reshape(LANES, WIN * LANES)
            for w in range(WIN):
                b = (a + w) % NY
                block = strip[:, w * LANES : (w + 1) * LANES]
                rfull[s, a * LANES : (a + 1) * LANES, b * LANES : (b + 1) * LANES] = block
                if 0 < w < WIN - 1:
                    rfull[s, b * LANES : (b + 1) * LANES, a * LANES : (a + 1) * LANES] = block.T

    def chips(k):
        return [wrap(y + k)] if k in (0, 4) else [wrap(y + k), wrap(y - k)]

    def chip_rows(s, k):
        return jnp.concatenate(
            [gall[s, pl.ds(2 * c, 2)].reshape(LANES, ORDER) for c in chips(k)], axis=0
        )

    def add_products(s, k):
        lhs = []
        for c in chips(k):
            here = pl.ds(pl.multiple_of(c * LANES, LANES), LANES)
            mine = pl.ds(pl.multiple_of(y * LANES, LANES), LANES)
            cols = gall[s, pl.ds(2 * c, 2), :, mine].reshape(LANES, LANES).T
            cols = jnp.where(core == 0, cols[:STRIP], cols[STRIP:])
            lhs.append(jnp.concatenate([lroot[s, :, here], cols], axis=0))
        lhs = jnp.concatenate(lhs, axis=1)
        rhs = chip_rows(s, k)
        for n in range(ORDER // TILE):
            tile = slice(n * TILE, (n + 1) * TILE)
            res = jnp.dot(lhs, rhs[:, tile], preferred_element_type=F32)
            if k == 0:
                half_acc[s, :, tile] = res[:STRIP]
                right_out[s, :, tile] = res[STRIP:]
            elif k < 4:
                half_acc[s, :, tile] += res[:STRIP]
                right_out[s, :, tile] += res[STRIP:]
            else:
                half[:, tile] = (half_acc[s, :, tile] + res[:STRIP]).astype(BF)
                right_out[s, :, tile] += res[STRIP:]

    def left_product(s, k):
        res = lax.dot_general(
            gall[s, d], chip_rows(s, k), (((1,), (1,)), ((), ())), preferred_element_type=F32
        )
        for j, c in enumerate(chips(k)):
            here = pl.ds(pl.multiple_of(c * LANES, LANES), LANES)
            left_out[s, :, here] = res[:, j * LANES : (j + 1) * LANES]

    def precondition(s):
        square = jnp.zeros((1, TILE), F32)
        near = [wrap(y + a) for a in range(NY)]
        lhs = jnp.concatenate(
            [half[:, pl.ds(pl.multiple_of(c * LANES, LANES), LANES)] for c in near], axis=1
        )
        for n in range(ORDER // TILE):
            tile = slice(n * TILE, (n + 1) * TILE)
            pre = jnp.dot(lhs, rfull[s, :, tile], preferred_element_type=F32)
            square += jnp.sum(pre * pre, axis=0, keepdims=True)
            for h in range(TILE // LANES):
                prec_m[near[n * (TILE // LANES) + h]] = pre[:, h * LANES : (h + 1) * LANES]
        norm[s, 0:1, :] = jnp.broadcast_to(jnp.sum(square, axis=1, keepdims=True), (1, LANES))

        @pl.loop(1, NDP)
        def _(i):
            n_copy(s, (d + i) % NDP, d).start()

        norms[s, d] = norm[s]
        for c in range(8):
            for r in range(2):
                strip_t[s, pl.ds(2 * c + r, NPREC, stride=Q), :] = prec_m[
                    c, pl.ds(r, NPREC, stride=2), :
                ]

    def factor(s):
        n_all(s).wait_recv()
        total = jnp.sum(norms[s], axis=0)
        return jnp.sqrt(total[1:2]) / (jnp.sqrt(total[0:1]) + 1e-06)

    def send_rows(s, rows):
        outgo[s] = rows.astype(BF).reshape(NPREC, Q, LANES)

        @pl.loop(1, NPREC)
        def _(i):
            e_copy(s, (p + i) % NPREC, p).start()

        back[SL * p + s] = outgo[s, p]

    def send_back(s):
        send_rows(s, strip_t[s] * factor(s))

    def f_copy(to, fro):
        return pltpu.make_async_remote_copy(
            src_ref=fac,
            dst_ref=facs.at[fro],
            send_sem=f_s,
            recv_sem=f_r,
            device_id=(d, to),
            device_id_type=MESH,
        )

    def f_all():
        ref = facs.at[pl.ds(0, NPREC - 1)]
        return pltpu.make_async_remote_copy(
            src_ref=ref, dst_ref=ref, send_sem=f_s, recv_sem=f_r,
            device_id=(other, p), device_id_type=MESH,
        )

    def out_copies(s):
        return [
            pltpu.make_async_copy(left_out.at[s], left_hbm.at[s], out_sem.at[0, s]),
            pltpu.make_async_copy(right_out.at[s], right_hbm.at[s], out_sem.at[1, s]),
        ]

    def grams(s, k):
        ring_other(gall, GD, s, k)
        add_products(s, k)
        left_product(s, k)

    def step(s, k):
        ring_step(gall, GR, GD, s, k)

    def finish(s):
        ring_other(gall, GD, s, 4)
        add_products(s, 4)
        precondition(s)
        left_product(s, 4)
        for copy in out_copies(s):
            copy.start()

    for s in range(SL):
        ring_step(wall, RR, RD, s, 1)
        whole_root(s, 0)
    for s in range(SL):
        ring_step(wall, RR, RD, s, 2)
        whole_root(s, 1)
    ring_step(wall, RR, RD, 0, 3)
    whole_root(0, 2)
    b_all().wait_recv()
    own_strip(0)
    ring_start(gall, GR, GD, 0)
    ring_step(wall, RR, RD, 1, 3)
    ring_step(wall, RR, RD, 2, 3)
    own_strip(1)
    whole_root(1, 2)
    step(0, 1)
    ring_start(gall, GR, GD, 1)
    own_strip(2)
    grams(0, 0)
    whole_root(2, 2)
    for s in range(SL):
        ring_step(wall, RR, RD, s, 4)
    step(0, 2)
    whole_root(0, 3)
    grams(0, 1)
    whole_root(0, 4)
    step(1, 1)
    grams(1, 0)
    grams(0, 2)
    step(0, 3)
    ring_start(gall, GR, GD, 2)
    whole_root(1, 3)
    grams(1, 1)
    grams(0, 3)
    step(1, 2)
    grams(2, 0)
    step(0, 4)
    step(2, 1)
    finish(0)
    step(1, 3)
    grams(1, 2)
    whole_root(1, 4)
    grams(2, 1)
    step(2, 2)
    send_back(0)
    grams(1, 3)
    step(1, 4)
    grams(2, 2)
    step(2, 3)
    finish(1)
    whole_root(2, 3)
    whole_root(2, 4)
    grams(2, 3)
    step(2, 4)
    ring_other(gall, GD, 2, 4)
    add_products(2, 4)
    precondition(2)
    send_rows(2, strip_t[2])
    send_back(1)
    left_product(2, 4)
    for copy in out_copies(2):
        copy.start()
    fac[...] = jnp.ones_like(fac)
    fac[2:3, :] = factor(2)

    @pl.loop(1, NPREC)
    def _(i):
        f_copy((p + i) % NPREC, p).start()

    facs[p] = fac[...]

    for s in range(SL):
        ring_drain(wall, RR, RD, s)
        ring_drain(gall, GR, GD, s)
        n_all(s).wait_send()
    for g in range(2):
        for t in range(5):
            sib_part(g, t).wait_send()
        for t in range(4):
            for h in range(2):
                if t or h == g:
                    rs_copy(g, t, h).wait_send()
    b_all().wait_send()
    for s in range(SL):
        e_all(s).wait_send()
        e_all(s).wait_recv()
    f_all().wait_send()
    f_all().wait_recv()

    @pl.loop(0, NB, unroll=8)
    def _(b):
        slot = table[b]
        scale = facs[lax.div(slot, SL), pl.ds(lax.rem(slot, SL), 1), :]
        upd_out[b] = (back[slot].astype(F32) * scale).astype(BF)

    last = pltpu.make_async_copy(upd_out, upd_hbm, out_sem.at[2, 0])
    last.start()
    for s in range(SL):
        for copy in out_copies(s):
            copy.wait()
    last.wait()


def hand_over(left_in, right_in, upd_in, left, right, upd, a, b, c, sem_in, sem_out):
    ins, outs = [], []
    for s in range(SL):
        for n, (src, mid, dst) in enumerate(((left_in, a, left), (right_in, b, right))):
            ins.append(pltpu.make_async_copy(src.at[s], mid.at[s], sem_in.at[n, s]))
            outs.append(pltpu.make_async_copy(mid.at[s], dst.at[s], sem_out.at[n, s]))
    ins.append(pltpu.make_async_copy(upd_in, c, sem_in.at[2, 0]))
    outs.append(pltpu.make_async_copy(c, upd, sem_out.at[2, 0]))
    for copy in ins:
        copy.start()
    for arrive, leave in zip(ins, outs):
        arrive.wait()
        leave.start()
    for copy in outs:
        copy.wait()


def body(grad_part, table, left_root, right_root):
    grad = grad_part.reshape(NB, NDP, 2, 8, LANES).transpose(0, 1, 3, 2, 4)
    grad = grad.reshape(NB, NDP, Q, LANES)
    slot = jnp.arange(SL * NPREC, dtype=jnp.int32)
    block = jnp.arange(1, NB + 1, dtype=jnp.int32)
    named = slot[:, None] == table[None, :]
    inv = jnp.sum(jnp.where(named, block[None, :], 0), axis=1, dtype=jnp.int32)
    vmem = pl.BlockSpec(memory_space=pltpu.VMEM)
    smem = pl.BlockSpec(memory_space=pltpu.SMEM)
    hbm = pl.BlockSpec(memory_space=pl.ANY)
    dma = pltpu.SemaphoreType.DMA
    results = [
        jax.ShapeDtypeStruct((SL, STRIP, ORDER), F32),
        jax.ShapeDtypeStruct((SL, STRIP, ORDER), F32),
        jax.ShapeDtypeStruct((NB, Q, LANES), BF),
    ]
    out = pl.pallas_call(
        kernel,
        out_shape=results,
        in_specs=[smem, smem, hbm, vmem, vmem],
        out_specs=[hbm, hbm, hbm],
        scratch_shapes=[
            pltpu.VMEM((NY, NB, Q, LANES), BF),
            pltpu.VMEM((NY, NB, Q, LANES), BF),
            pltpu.VMEM((2, 4, NB, Q, LANES), BF),
            pltpu.VMEM((NB + 1, Q, LANES), BF),
            pltpu.VMEM((SL * NPREC, Q, LANES), BF),
            pltpu.VMEM((NPREC, SL, Q, LANES), BF),
            pltpu.VMEM((SL, NPREC * Q, LANES), F32),
            pltpu.VMEM((8, STRIP, LANES), F32),
            pltpu.VMEM((SL, NDP, STRIP, ORDER), BF),
            pltpu.VMEM((SL, NDP, STRIP, WIN * LANES), BF),
            pltpu.VMEM((SL, ORDER, ORDER), BF),
            pltpu.VMEM((SL, STRIP, ORDER), F32),
            pltpu.VMEM((STRIP, ORDER), BF),
            pltpu.VMEM((8, STRIP, LANES), F32),
            pltpu.VMEM((SL, NPREC, Q, LANES), BF),
            pltpu.VMEM((SL * NPREC, Q, LANES), BF),
            pltpu.VMEM((SL, 8, LANES), F32),
            pltpu.VMEM((SL, NDP, 8, LANES), F32),
            pltpu.VMEM((8, LANES), F32),
            pltpu.VMEM((NPREC, 8, LANES), F32),
            pltpu.VMEM((SL, STRIP, ORDER), F32),
            pltpu.VMEM((SL, STRIP, ORDER), F32),
            pltpu.VMEM((NB, Q, LANES), BF),
            dma((2, 5)), dma((2, 5)), dma((2, 5)),
            dma((2, 4, 2)), dma((2, 4, 2)),
            dma, dma,
            dma((SL, 2, 4)), dma((SL, 2, 4)), dma((SL, 9)), dma((SL, 9)),
            dma((SL, 2, 4)), dma((SL, 2, 4)), dma((SL, 9)), dma((SL, 9)),
            dma((SL,)), dma((SL,)),
            dma((SL,)), dma((SL,)),
            dma, dma,
            dma((3, SL)),
        ],
        compiler_params=pltpu.CompilerParams(
            collective_id=0, has_side_effects=True, vmem_limit_bytes=56 * 2**20
        ),
        cost_estimate=pl.CostEstimate(
            flops=2 * SL * 5 * STRIP * ORDER * ORDER, bytes_accessed=8 * 2**20, transcendentals=0
        ),
        name="shampoo_step",
    )(inv, table, grad, left_root, right_root)
    left, right, upd = pl.pallas_call(
        hand_over,
        out_shape=results,
        in_specs=[hbm, hbm, hbm],
        out_specs=[hbm, hbm, hbm],
        scratch_shapes=[
            pltpu.VMEM((SL, STRIP, ORDER), F32),
            pltpu.VMEM((SL, STRIP, ORDER), F32),
            pltpu.VMEM((NB, Q, LANES), BF),
            dma((3, SL)),
            dma((3, SL)),
        ],
        compiler_params=pltpu.CompilerParams(vmem_limit_bytes=56 * 2**20),
        name="hand_over",
    )(*out)
    update = upd.reshape(NB, 8, 2, LANES).transpose(0, 2, 1, 3).reshape(NB, 1, 1, 2, ORDER)
    return (left, right, update)


def solution(mesh):
    in_specs = (
        P("dp", None, None, "prec", None, None),
        P(),
        P("prec", "dp", None),
        P("prec", "dp", None),
    )
    out_specs = (P("prec", "dp", None), P("prec", "dp", None), P(None, "dp", "prec", None, None))
    return jax.shard_map(body, mesh=mesh, in_specs=in_specs, out_specs=out_specs, check_vma=False)
```

```python
import jax
import jax.numpy as jnp
from jax import lax
from jax.experimental import pallas as pl
from jax.experimental.pallas import tpu as pltpu
from jax.sharding import PartitionSpec as P

MESH = pl.DeviceIdType.MESH
BF = jnp.bfloat16
F32 = jnp.float32

NY = 8
NDP = 16
NPREC = 32
SL = 3
NB = 40
STRIP = 64
ORDER = 1024
LANES = 128
Q = 16
HALF = NB // 2
WIN = 5
TILE = 256
SIGNS = (1, -1)


def kernel(
    inv, table, grad, lroot, rroot, left_hbm, right_hbm, upd_hbm,
    part, sib, ringbuf, summed, slots, got, strip_t, strip_m, gall, wall, rfull,
    half_acc, half, prec_m, outgo, back, norm, norms, fac, facs, left_out, right_out, upd_out,
    part_sem, sib_s, sib_r, rs_s, rs_r, b_s, b_r,
    rr_s, rr_r, rd_s, rd_r, gr_s, gr_r, gd_s, gd_r,
    e_s, e_r, n_s, n_r, f_s, f_r, out_sem,
):
    d = lax.axis_index("dp")
    p = lax.axis_index("prec")
    y = d // 2
    core = d % 2
    other = 2 * y + (1 - core)

    def wrap(v):
        return lax.rem(v + NY, NY)

    def dp_of(chip_y):
        return 2 * chip_y + core

    barrier = pltpu.get_barrier_semaphore()

    @pl.loop(1, NDP)
    def _(i):
        pl.semaphore_signal(barrier, inc=1, device_id=(lax.rem(d + i, NDP), p), device_id_type=MESH)

    @pl.loop(1, NPREC)
    def _(i):
        pl.semaphore_signal(barrier, inc=1, device_id=(d, lax.rem(p + i, NPREC)), device_id_type=MESH)

    def chunk(g, t):
        return wrap(y + SIGNS[g] * (4 - t))

    def share(g, t):
        return pl.ds(g * HALF, HALF) if t in (0, 4) else pl.ds(0, NB)

    def local_part(g, t):
        c = chunk(g, t)
        return pltpu.make_async_copy(
            grad.at[share(g, t), 2 * c + core], part.at[c, share(g, t)], part_sem.at[g, t]
        )

    def sib_part(g, t):
        c = chunk(g, t)
        return pltpu.make_async_remote_copy(
            src_ref=grad.at[share(g, t), 2 * c + (1 - core)],
            dst_ref=sib.at[c, share(g, t)],
            send_sem=sib_s.at[g, t],
            recv_sem=sib_r.at[g, t],
            device_id=(other, p),
            device_id_type=MESH,
        )

    for t in range(5):
        for g in range(2):
            local_part(g, t).start()

    for w in range(WIN):
        cols = pl.ds(pl.multiple_of(wrap(y + w) * LANES, LANES), LANES)
        for s in range(SL):
            wall[s, d, :, w * LANES : (w + 1) * LANES] = rroot[s, :, cols]

    pl.semaphore_wait(barrier, NDP + NPREC - 2)
    for t in range(5):
        for g in range(2):
            sib_part(g, t).start()

    def hop(buf, ss, rs, s, g, k):
        o = wrap(y - SIGNS[g] * (k - 1))
        rows = pl.ds(0, STRIP) if k < 4 else pl.ds(g * (STRIP // 2), STRIP // 2)
        ref = buf.at[s, dp_of(o), rows]
        return pltpu.make_async_remote_copy(
            src_ref=ref,
            dst_ref=ref,
            send_sem=ss.at[s, g, k - 1],
            recv_sem=rs.at[s, g, k - 1],
            device_id=(dp_of(wrap(y + SIGNS[g])), p),
            device_id_type=MESH,
        )

    def landing(buf, ss, rs, s, g, k):
        o = wrap(y - SIGNS[g] * k)
        rows = pl.ds(0, STRIP) if k < 4 else pl.ds(g * (STRIP // 2), STRIP // 2)
        ref = buf.at[s, dp_of(o), rows]
        return pltpu.make_async_remote_copy(
            src_ref=ref,
            dst_ref=ref,
            send_sem=ss.at[s, g, k - 1],
            recv_sem=rs.at[s, g, k - 1],
            device_id=(dp_of(wrap(y + SIGNS[g])), p),
            device_id_type=MESH,
        )

    def across(buf, ss, rs, s, g, k, mine):
        o = wrap(y - SIGNS[g] * k)
        rows = pl.ds(0, STRIP) if k < 4 else pl.ds(g * (STRIP // 2), STRIP // 2)
        ref = buf.at[s, 2 * o + (core if mine else 1 - core), rows]
        n = 0 if k == 0 else 1 + g * 4 + (k - 1)
        return pltpu.make_async_remote_copy(
            src_ref=ref,
            dst_ref=ref,
            send_sem=ss.at[s, n],
            recv_sem=rs.at[s, n],
            device_id=(other, p),
            device_id_type=MESH,
        )

    def ring_start(buf, rsem, dsem, s):
        for g in range(2):
            hop(buf, *rsem, s, g, 1).start()
        across(buf, *dsem, s, 0, 0, True).start()

    def ring_step(buf, rsem, dsem, s, k):
        for g in range(2):
            landing(buf, *rsem, s, g, k).wait_recv()
            if k < 4:
                hop(buf, *rsem, s, g, k + 1).start()
            across(buf, *dsem, s, g, k, True).start()

    def ring_other(buf, dsem, s, k):
        for g in range(2 if k else 1):
            across(buf, *dsem, s, g, k, False).wait_recv()

    def ring_drain(buf, rsem, dsem, s):
        for k in range(5):
            for g in range(2 if k else 1):
                if k:
                    hop(buf, *rsem, s, g, k).wait_send()
                across(buf, *dsem, s, g, k, True).wait_send()

    RR, RD, GR, GD = (rr_s, rr_r), (rd_s, rd_r), (gr_s, gr_r), (gd_s, gd_r)

    def rs_copy(g, t, h):
        return pltpu.make_async_remote_copy(
            src_ref=part.at[chunk(g, t), pl.ds(h * HALF, HALF)],
            dst_ref=ringbuf.at[g, t, pl.ds(h * HALF, HALF)],
            send_sem=rs_s.at[g, t, h],
            recv_sem=rs_r.at[g, t, h],
            device_id=(dp_of(wrap(y + SIGNS[g])), p),
            device_id_type=MESH,
        )

    def rs_step(g, t, h):
        blocks = pl.ds(h * HALF, HALF)
        c = chunk(g, t)
        total = part[c, blocks].astype(F32) + sib[c, blocks].astype(F32)
        if t > 1 or (t == 1 and h == g):
            rs_copy(g, t - 1, h).wait_recv()
            total += ringbuf[g, t - 1, blocks].astype(F32)
        part[c, blocks] = total.astype(BF)
        rs_copy(g, t, h).start()

    def rs_ready(t):
        for g in range(2):
            local_part(g, t).wait()
            sib_part(g, t).wait_recv()

    ring_start(wall, RR, RD, 0)
    rs_ready(0)
    for g in range(2):
        rs_step(g, 0, g)
    for t in range(1, 4):
        rs_ready(t)
        for g in range(2):
            rs_step(g, t, 1 - g)
        for g in range(2):
            rs_step(g, t, g)
    ring_start(wall, RR, RD, 1)
    for h in range(2):
        local_part(h, 4).wait()
        sib_part(h, 4).wait_recv()
        blocks = pl.ds(h * HALF, HALF)
        total = part[y, blocks].astype(F32) + sib[y, blocks].astype(F32)
        for g in range(2):
            rs_copy(g, 3, h).wait_recv()
            total += ringbuf[g, 3, blocks].astype(F32)
        summed[pl.ds(1 + h * HALF, HALF)] = total.astype(BF)
    summed[0] = jnp.zeros((Q, LANES), BF)

    @pl.loop(0, SL * NPREC, unroll=8)
    def _(s):
        slots[s] = summed[inv[s]]

    def b_copy(to, fro):
        return pltpu.make_async_remote_copy(
            src_ref=slots.at[pl.ds(SL * to, SL)],
            dst_ref=got.at[fro],
            send_sem=b_s,
            recv_sem=b_r,
            device_id=(d, to),
            device_id_type=MESH,
        )

    def b_all():
        ref = got.at[pl.ds(0, NPREC - 1)]
        return pltpu.make_async_remote_copy(
            src_ref=ref, dst_ref=ref, send_sem=b_s, recv_sem=b_r,
            device_id=(other, p), device_id_type=MESH,
        )

    def e_copy(s, to, fro):
        return pltpu.make_async_remote_copy(
            src_ref=outgo.at[s, to],
            dst_ref=back.at[SL * fro + s],
            send_sem=e_s.at[s],
            recv_sem=e_r.at[s],
            device_id=(d, to),
            device_id_type=MESH,
        )

    def e_all(s):
        ref = outgo.at[s, pl.ds(0, NPREC - 1)]
        return pltpu.make_async_remote_copy(
            src_ref=ref, dst_ref=ref, send_sem=e_s.at[s], recv_sem=e_r.at[s],
            device_id=(other, p), device_id_type=MESH,
        )

    def n_copy(to, fro):
        return pltpu.make_async_remote_copy(
            src_ref=norm,
            dst_ref=norms.at[fro],
            send_sem=n_s,
            recv_sem=n_r,
            device_id=(to, p),
            device_id_type=MESH,
        )

    def n_all():
        ref = norms.at[pl.ds(0, NDP - 1)]
        return pltpu.make_async_remote_copy(
            src_ref=ref, dst_ref=ref, send_sem=n_s, recv_sem=n_r,
            device_id=(other, p), device_id_type=MESH,
        )

    @pl.loop(1, NPREC)
    def _(i):
        b_copy(lax.rem(p + i, NPREC), p).start()

    got[p] = slots[pl.ds(SL * p, SL)]

    ring_start(wall, RR, RD, 2)

    norm[...] = jnp.zeros_like(norm)

    def own_strip(s):
        rows = got[:, s].astype(F32).reshape(NPREC * Q, LANES)
        strip_t[s] = rows
        square = jnp.sum(jnp.sum(rows * rows, axis=0, keepdims=True), axis=1, keepdims=True)
        norm[8 + s : 9 + s, :] = jnp.broadcast_to(square, (1, LANES))
        for c in range(8):
            for r in range(2):
                strip_m[c, pl.ds(r, NPREC, stride=2), :] = strip_t[
                    s, pl.ds(2 * c + r, NPREC, stride=Q), :
                ]
        for c in range(8):
            gall[s, d, :, c * LANES : (c + 1) * LANES] = strip_m[c].astype(BF)

    def whole_root(s, k):
        ring_other(wall, RD, s, k)
        for a in sorted({k, (NY - k) % NY}):
            strip = wall[s, pl.ds(2 * wrap(y + a), 2)].reshape(LANES, WIN * LANES)
            for w in range(WIN):
                b = (a + w) % NY
                block = strip[:, w * LANES : (w + 1) * LANES]
                rfull[s, a * LANES : (a + 1) * LANES, b * LANES : (b + 1) * LANES] = block
                if 0 < w < WIN - 1:
                    rfull[s, b * LANES : (b + 1) * LANES, a * LANES : (a + 1) * LANES] = block.T

    def chips(k):
        return [wrap(y + k)] if k in (0, 4) else [wrap(y + k), wrap(y - k)]

    def chip_rows(s, k):
        return jnp.concatenate(
            [gall[s, pl.ds(2 * c, 2)].reshape(LANES, ORDER) for c in chips(k)], axis=0
        )

    def add_products(s, k):
        lhs = []
        for c in chips(k):
            here = pl.ds(pl.multiple_of(c * LANES, LANES), LANES)
            mine = pl.ds(pl.multiple_of(y * LANES, LANES), LANES)
            cols = gall[s, pl.ds(2 * c, 2), :, mine].reshape(LANES, LANES).T
            cols = jnp.where(core == 0, cols[:STRIP], cols[STRIP:])
            lhs.append(jnp.concatenate([lroot[s, :, here], cols], axis=0))
        lhs = jnp.concatenate(lhs, axis=1)
        rhs = chip_rows(s, k)
        for n in range(ORDER // TILE):
            tile = slice(n * TILE, (n + 1) * TILE)
            res = jnp.dot(lhs, rhs[:, tile], preferred_element_type=F32)
            if k == 0:
                half_acc[s, :, tile] = res[:STRIP]
                right_out[s, :, tile] = res[STRIP:]
            elif k < 4:
                half_acc[s, :, tile] += res[:STRIP]
                right_out[s, :, tile] += res[STRIP:]
            else:
                half[:, tile] = (half_acc[s, :, tile] + res[:STRIP]).astype(BF)
                right_out[s, :, tile] += res[STRIP:]

    def left_product(s, k):
        res = lax.dot_general(
            gall[s, d], chip_rows(s, k), (((1,), (1,)), ((), ())), preferred_element_type=F32
        )
        for j, c in enumerate(chips(k)):
            here = pl.ds(pl.multiple_of(c * LANES, LANES), LANES)
            left_out[s, :, here] = res[:, j * LANES : (j + 1) * LANES]

    def precondition(s):
        square = jnp.zeros((1, TILE), F32)
        near = [wrap(y + a) for a in range(NY)]
        lhs = jnp.concatenate(
            [half[:, pl.ds(pl.multiple_of(c * LANES, LANES), LANES)] for c in near], axis=1
        )
        for n in range(ORDER // TILE):
            tile = slice(n * TILE, (n + 1) * TILE)
            pre = jnp.dot(lhs, rfull[s, :, tile], preferred_element_type=F32)
            square += jnp.sum(pre * pre, axis=0, keepdims=True)
            for h in range(TILE // LANES):
                prec_m[near[n * (TILE // LANES) + h]] = pre[:, h * LANES : (h + 1) * LANES]
        norm[s : s + 1, :] = jnp.broadcast_to(jnp.sum(square, axis=1, keepdims=True), (1, LANES))

    def send_norms():
        @pl.loop(1, NDP)
        def _(i):
            n_copy(lax.rem(d + i, NDP), d).start()

        norms[d] = norm[...]

    def send_rows(s):
        for c in range(8):
            for r in range(2):
                strip_t[s, pl.ds(2 * c + r, NPREC, stride=Q), :] = prec_m[
                    c, pl.ds(r, NPREC, stride=2), :
                ]
        outgo[s] = strip_t[s].astype(BF).reshape(NPREC, Q, LANES)

        @pl.loop(1, NPREC)
        def _(i):
            e_copy(s, lax.rem(p + i, NPREC), p).start()

        back[SL * p + s] = outgo[s, p]

    def f_copy(to, fro):
        return pltpu.make_async_remote_copy(
            src_ref=fac,
            dst_ref=facs.at[fro],
            send_sem=f_s,
            recv_sem=f_r,
            device_id=(d, to),
            device_id_type=MESH,
        )

    def f_all():
        ref = facs.at[pl.ds(0, NPREC - 1)]
        return pltpu.make_async_remote_copy(
            src_ref=ref, dst_ref=ref, send_sem=f_s, recv_sem=f_r,
            device_id=(other, p), device_id_type=MESH,
        )

    def out_copies(s):
        return [
            pltpu.make_async_copy(left_out.at[s], left_hbm.at[s], out_sem.at[0, s]),
            pltpu.make_async_copy(right_out.at[s], right_hbm.at[s], out_sem.at[1, s]),
        ]

    def grams(s, k):
        ring_other(gall, GD, s, k)
        add_products(s, k)
        left_product(s, k)

    def step(s, k):
        ring_step(gall, GR, GD, s, k)

    def finish(s):
        ring_other(gall, GD, s, 4)
        add_products(s, 4)
        precondition(s)
        if s == SL - 1:
            send_norms()
        send_rows(s)
        left_product(s, 4)
        for copy in out_copies(s):
            copy.start()

    for s in range(SL):
        ring_step(wall, RR, RD, s, 1)
        whole_root(s, 0)
    for s in range(SL):
        ring_step(wall, RR, RD, s, 2)
        whole_root(s, 1)
    ring_step(wall, RR, RD, 0, 3)
    whole_root(0, 2)
    b_all().wait_recv()
    own_strip(0)
    ring_start(gall, GR, GD, 0)
    ring_step(wall, RR, RD, 1, 3)
    ring_step(wall, RR, RD, 2, 3)
    own_strip(1)
    ring_start(gall, GR, GD, 1)
    whole_root(1, 2)
    own_strip(2)
    whole_root(2, 2)
    whole_root(0, 3)
    step(0, 1)
    whole_root(1, 3)
    for s in range(SL):
        ring_step(wall, RR, RD, s, 4)
    grams(0, 0)
    whole_root(2, 3)
    step(1, 1)
    grams(1, 0)
    step(0, 2)
    whole_root(0, 4)
    grams(0, 1)
    ring_start(gall, GR, GD, 2)
    grams(1, 1)
    step(1, 2)
    grams(0, 2)
    step(0, 3)
    whole_root(1, 4)
    grams(2, 0)
    grams(1, 2)
    step(2, 1)
    grams(0, 3)
    step(1, 3)
    step(0, 4)
    grams(2, 1)
    finish(0)
    step(2, 2)
    grams(1, 3)
    step(1, 4)
    grams(2, 2)
    step(2, 3)
    finish(1)
    whole_root(2, 4)
    grams(2, 3)
    step(2, 4)
    finish(2)
    n_all().wait_recv()
    total = jnp.sum(norms[...], axis=0)
    fac[...] = jnp.sqrt(total[8:16]) / (jnp.sqrt(total[0:8]) + 1e-06)

    @pl.loop(1, NPREC)
    def _(i):
        f_copy(lax.rem(p + i, NPREC), p).start()

    facs[p] = fac[...]

    for s in range(SL):
        ring_drain(wall, RR, RD, s)
        ring_drain(gall, GR, GD, s)
    for g in range(2):
        for t in range(5):
            sib_part(g, t).wait_send()
        for t in range(4):
            for h in range(2):
                if t or h == g:
                    rs_copy(g, t, h).wait_send()
    b_all().wait_send()
    n_all().wait_send()
    for s in range(SL):
        e_all(s).wait_send()
        e_all(s).wait_recv()
    f_all().wait_send()
    f_all().wait_recv()

    @pl.loop(0, NB, unroll=8)
    def _(b):
        slot = table[b]
        scale = facs[lax.div(slot, SL), pl.ds(lax.rem(slot, SL), 1), :]
        upd_out[b] = (back[slot].astype(F32) * scale).astype(BF)

    last = pltpu.make_async_copy(upd_out, upd_hbm, out_sem.at[2, 0])
    last.start()
    for s in range(SL):
        for copy in out_copies(s):
            copy.wait()
    last.wait()


def hand_over(left_in, right_in, upd_in, left, right, upd, a, b, c, sem_in, sem_out):
    ins, outs = [], []
    for s in range(SL):
        for n, (src, mid, dst) in enumerate(((left_in, a, left), (right_in, b, right))):
            ins.append(pltpu.make_async_copy(src.at[s], mid.at[s], sem_in.at[n, s]))
            outs.append(pltpu.make_async_copy(mid.at[s], dst.at[s], sem_out.at[n, s]))
    ins.append(pltpu.make_async_copy(upd_in, c, sem_in.at[2, 0]))
    outs.append(pltpu.make_async_copy(c, upd, sem_out.at[2, 0]))
    for copy in ins:
        copy.start()
    for arrive, leave in zip(ins, outs):
        arrive.wait()
        leave.start()
    for copy in outs:
        copy.wait()


def body(grad_part, table, left_root, right_root):
    grad = grad_part.reshape(NB, NDP, 2, 8, LANES).transpose(0, 1, 3, 2, 4)
    grad = grad.reshape(NB, NDP, Q, LANES)
    slot = jnp.arange(SL * NPREC, dtype=jnp.int32)
    block = jnp.arange(1, NB + 1, dtype=jnp.int32)
    named = slot[:, None] == table[None, :]
    inv = jnp.sum(jnp.where(named, block[None, :], 0), axis=1, dtype=jnp.int32)
    vmem = pl.BlockSpec(memory_space=pltpu.VMEM)
    smem = pl.BlockSpec(memory_space=pltpu.SMEM)
    hbm = pl.BlockSpec(memory_space=pl.ANY)
    dma = pltpu.SemaphoreType.DMA
    results = [
        jax.ShapeDtypeStruct((SL, STRIP, ORDER), F32),
        jax.ShapeDtypeStruct((SL, STRIP, ORDER), F32),
        jax.ShapeDtypeStruct((NB, Q, LANES), BF),
    ]
    out = pl.pallas_call(
        kernel,
        out_shape=results,
        in_specs=[smem, smem, hbm, vmem, vmem],
        out_specs=[hbm, hbm, hbm],
        scratch_shapes=[
            pltpu.VMEM((NY, NB, Q, LANES), BF),
            pltpu.VMEM((NY, NB, Q, LANES), BF),
            pltpu.VMEM((2, 4, NB, Q, LANES), BF),
            pltpu.VMEM((NB + 1, Q, LANES), BF),
            pltpu.VMEM((SL * NPREC, Q, LANES), BF),
            pltpu.VMEM((NPREC, SL, Q, LANES), BF),
            pltpu.VMEM((SL, NPREC * Q, LANES), F32),
            pltpu.VMEM((8, STRIP, LANES), F32),
            pltpu.VMEM((SL, NDP, STRIP, ORDER), BF),
            pltpu.VMEM((SL, NDP, STRIP, WIN * LANES), BF),
            pltpu.VMEM((SL, ORDER, ORDER), BF),
            pltpu.VMEM((SL, STRIP, ORDER), F32),
            pltpu.VMEM((STRIP, ORDER), BF),
            pltpu.VMEM((8, STRIP, LANES), F32),
            pltpu.VMEM((SL, NPREC, Q, LANES), BF),
            pltpu.VMEM((SL * NPREC, Q, LANES), BF),
            pltpu.VMEM((16, LANES), F32),
            pltpu.VMEM((NDP, 16, LANES), F32),
            pltpu.VMEM((8, LANES), F32),
            pltpu.VMEM((NPREC, 8, LANES), F32),
            pltpu.VMEM((SL, STRIP, ORDER), F32),
            pltpu.VMEM((SL, STRIP, ORDER), F32),
            pltpu.VMEM((NB, Q, LANES), BF),
            dma((2, 5)), dma((2, 5)), dma((2, 5)),
            dma((2, 4, 2)), dma((2, 4, 2)),
            dma, dma,
            dma((SL, 2, 4)), dma((SL, 2, 4)), dma((SL, 9)), dma((SL, 9)),
            dma((SL, 2, 4)), dma((SL, 2, 4)), dma((SL, 9)), dma((SL, 9)),
            dma((SL,)), dma((SL,)),
            dma, dma,
            dma, dma,
            dma((3, SL)),
        ],
        compiler_params=pltpu.CompilerParams(
            collective_id=0, has_side_effects=True, vmem_limit_bytes=56 * 2**20
        ),
        cost_estimate=pl.CostEstimate(
            flops=2 * SL * 5 * STRIP * ORDER * ORDER, bytes_accessed=8 * 2**20, transcendentals=0
        ),
        name="shampoo_step",
    )(inv, table, grad, left_root, right_root)
    left, right, upd = pl.pallas_call(
        hand_over,
        out_shape=results,
        in_specs=[hbm, hbm, hbm],
        out_specs=[hbm, hbm, hbm],
        scratch_shapes=[
            pltpu.VMEM((SL, STRIP, ORDER), F32),
            pltpu.VMEM((SL, STRIP, ORDER), F32),
            pltpu.VMEM((NB, Q, LANES), BF),
            dma((3, SL)),
            dma((3, SL)),
        ],
        compiler_params=pltpu.CompilerParams(vmem_limit_bytes=56 * 2**20),
        name="hand_over",
    )(*out)
    update = upd.reshape(NB, 8, 2, LANES).transpose(0, 2, 1, 3).reshape(NB, 1, 1, 2, ORDER)
    return (left, right, update)


def solution(mesh):
    in_specs = (
        P("dp", None, None, "prec", None, None),
        P(),
        P("prec", "dp", None),
        P("prec", "dp", None),
    )
    out_specs = (P("prec", "dp", None), P("prec", "dp", None), P(None, "dp", "prec", None, None))
    return jax.shard_map(body, mesh=mesh, in_specs=in_specs, out_specs=out_specs, check_vma=False)
```

```python
import jax
import jax.numpy as jnp
from jax import lax
from jax.experimental import pallas as pl
from jax.experimental.pallas import tpu as pltpu
from jax.sharding import PartitionSpec as P

MESH = pl.DeviceIdType.MESH
BF = jnp.bfloat16
F32 = jnp.float32

NY = 8
NDP = 16
NPREC = 32
SL = 3
NB = 40
STRIP = 64
ORDER = 1024
LANES = 128
Q = 16
HALF = NB // 2
WIN = 5
TILE = 256
SIGNS = (1, -1)


def kernel(
    inv, table, grad, lroot, rroot, left_hbm, right_hbm, upd_hbm,
    part, sib, ringbuf, summed, slots, got, strip_t, strip_m, gall, wall, rfull,
    half_acc, half, prec_m, outgo, back, norm, norms, fac, facs, left_out, right_out, upd_out,
    part_sem, sib_s, sib_r, rs_s, rs_r, b_s, b_r,
    rr_s, rr_r, rd_s, rd_r, gr_s, gr_r, gd_s, gd_r,
    e_s, e_r, n_s, n_r, f_s, f_r, out_sem,
):
    d = lax.axis_index("dp")
    p = lax.axis_index("prec")
    y = d // 2
    core = d % 2
    other = 2 * y + (1 - core)

    def wrap(v):
        return lax.rem(v + NY, NY)

    def dp_of(chip_y):
        return 2 * chip_y + core

    barrier = pltpu.get_barrier_semaphore()

    @pl.loop(1, NDP)
    def _(i):
        pl.semaphore_signal(barrier, inc=1, device_id=(lax.rem(d + i, NDP), p), device_id_type=MESH)

    @pl.loop(1, NPREC)
    def _(i):
        pl.semaphore_signal(barrier, inc=1, device_id=(d, lax.rem(p + i, NPREC)), device_id_type=MESH)

    def chunk(g, t):
        return wrap(y + SIGNS[g] * (4 - t))

    def share(g, t):
        return pl.ds(g * HALF, HALF) if t in (0, 4) else pl.ds(0, NB)

    def local_part(g, t):
        c = chunk(g, t)
        return pltpu.make_async_copy(
            grad.at[share(g, t), 2 * c + core], part.at[c, share(g, t)], part_sem.at[g, t]
        )

    def sib_part(g, t):
        c = chunk(g, t)
        return pltpu.make_async_remote_copy(
            src_ref=grad.at[share(g, t), 2 * c + (1 - core)],
            dst_ref=sib.at[c, share(g, t)],
            send_sem=sib_s.at[g, t],
            recv_sem=sib_r.at[g, t],
            device_id=(other, p),
            device_id_type=MESH,
        )

    for t in range(5):
        for g in range(2):
            local_part(g, t).start()

    for w in range(WIN):
        cols = pl.ds(pl.multiple_of(wrap(y + w) * LANES, LANES), LANES)
        for s in range(SL):
            wall[s, d, :, w * LANES : (w + 1) * LANES] = rroot[s, :, cols]

    pl.semaphore_wait(barrier, NDP + NPREC - 2)
    for t in range(5):
        for g in range(2):
            sib_part(g, t).start()

    def ring_copy(buf, ss, rs, s, g, k, h, o):
        ref = buf.at[s, dp_of(o), pl.ds(h * (STRIP // 2), STRIP // 2)]
        return pltpu.make_async_remote_copy(
            src_ref=ref,
            dst_ref=ref,
            send_sem=ss.at[s, g, k - 1, h],
            recv_sem=rs.at[s, g, k - 1, h],
            device_id=(dp_of(wrap(y + SIGNS[g])), p),
            device_id_type=MESH,
        )

    def hop(buf, ss, rs, s, g, k, h):
        return ring_copy(buf, ss, rs, s, g, k, h, wrap(y - SIGNS[g] * (k - 1)))

    def landing(buf, ss, rs, s, g, k, h):
        return ring_copy(buf, ss, rs, s, g, k, h, wrap(y - SIGNS[g] * k))

    def halves(g, k):
        return (g, 1 - g) if k < 4 else (g,)

    def across(buf, ss, rs, s, g, k, mine):
        o = wrap(y - SIGNS[g] * k)
        rows = pl.ds(0, STRIP) if k < 4 else pl.ds(g * (STRIP // 2), STRIP // 2)
        ref = buf.at[s, 2 * o + (core if mine else 1 - core), rows]
        n = 0 if k == 0 else 1 + g * 4 + (k - 1)
        return pltpu.make_async_remote_copy(
            src_ref=ref,
            dst_ref=ref,
            send_sem=ss.at[s, n],
            recv_sem=rs.at[s, n],
            device_id=(other, p),
            device_id_type=MESH,
        )

    def ring_start(buf, rsem, dsem, s):
        for n in range(2):
            for g in range(2):
                hop(buf, *rsem, s, g, 1, halves(g, 1)[n]).start()
        across(buf, *dsem, s, 0, 0, True).start()

    def ring_step(buf, rsem, dsem, s, k):
        for n in range(len(halves(0, k))):
            for g in range(2):
                h = halves(g, k)[n]
                landing(buf, *rsem, s, g, k, h).wait_recv()
                if k < 4 and h in halves(g, k + 1):
                    hop(buf, *rsem, s, g, k + 1, h).start()
        for g in range(2):
            across(buf, *dsem, s, g, k, True).start()

    def ring_other(buf, dsem, s, k):
        for g in range(2 if k else 1):
            across(buf, *dsem, s, g, k, False).wait_recv()

    def ring_drain(buf, rsem, dsem, s):
        for k in range(5):
            for g in range(2 if k else 1):
                for h in halves(g, k) if k else ():
                    hop(buf, *rsem, s, g, k, h).wait_send()
                across(buf, *dsem, s, g, k, True).wait_send()

    RR, RD, GR, GD = (rr_s, rr_r), (rd_s, rd_r), (gr_s, gr_r), (gd_s, gd_r)

    def rs_copy(g, t, h):
        return pltpu.make_async_remote_copy(
            src_ref=part.at[chunk(g, t), pl.ds(h * HALF, HALF)],
            dst_ref=ringbuf.at[g, t, pl.ds(h * HALF, HALF)],
            send_sem=rs_s.at[g, t, h],
            recv_sem=rs_r.at[g, t, h],
            device_id=(dp_of(wrap(y + SIGNS[g])), p),
            device_id_type=MESH,
        )

    def rs_step(g, t, h):
        blocks = pl.ds(h * HALF, HALF)
        c = chunk(g, t)
        total = part[c, blocks].astype(F32) + sib[c, blocks].astype(F32)
        if t > 1 or (t == 1 and h == g):
            rs_copy(g, t - 1, h).wait_recv()
            total += ringbuf[g, t - 1, blocks].astype(F32)
        part[c, blocks] = total.astype(BF)
        rs_copy(g, t, h).start()

    def rs_ready(t):
        for g in range(2):
            local_part(g, t).wait()
            sib_part(g, t).wait_recv()

    ring_start(wall, RR, RD, 0)
    rs_ready(0)
    for g in range(2):
        rs_step(g, 0, g)
    for t in range(1, 4):
        rs_ready(t)
        for g in range(2):
            rs_step(g, t, 1 - g)
        for g in range(2):
            rs_step(g, t, g)
    ring_start(wall, RR, RD, 1)
    for h in range(2):
        local_part(h, 4).wait()
        sib_part(h, 4).wait_recv()
        blocks = pl.ds(h * HALF, HALF)
        total = part[y, blocks].astype(F32) + sib[y, blocks].astype(F32)
        for g in range(2):
            rs_copy(g, 3, h).wait_recv()
            total += ringbuf[g, 3, blocks].astype(F32)
        summed[pl.ds(1 + h * HALF, HALF)] = total.astype(BF)
    summed[0] = jnp.zeros((Q, LANES), BF)

    @pl.loop(0, SL * NPREC, unroll=8)
    def _(s):
        slots[s] = summed[inv[s]]

    def b_copy(to, fro):
        return pltpu.make_async_remote_copy(
            src_ref=slots.at[pl.ds(SL * to, SL)],
            dst_ref=got.at[fro],
            send_sem=b_s,
            recv_sem=b_r,
            device_id=(d, to),
            device_id_type=MESH,
        )

    def b_all():
        ref = got.at[pl.ds(0, NPREC - 1)]
        return pltpu.make_async_remote_copy(
            src_ref=ref, dst_ref=ref, send_sem=b_s, recv_sem=b_r,
            device_id=(other, p), device_id_type=MESH,
        )

    def e_copy(s, to, fro):
        return pltpu.make_async_remote_copy(
            src_ref=outgo.at[s, to],
            dst_ref=back.at[SL * fro + s],
            send_sem=e_s.at[s],
            recv_sem=e_r.at[s],
            device_id=(d, to),
            device_id_type=MESH,
        )

    def e_all(s):
        ref = outgo.at[s, pl.ds(0, NPREC - 1)]
        return pltpu.make_async_remote_copy(
            src_ref=ref, dst_ref=ref, send_sem=e_s.at[s], recv_sem=e_r.at[s],
            device_id=(other, p), device_id_type=MESH,
        )

    def n_copy(to, fro):
        return pltpu.make_async_remote_copy(
            src_ref=norm,
            dst_ref=norms.at[fro],
            send_sem=n_s,
            recv_sem=n_r,
            device_id=(to, p),
            device_id_type=MESH,
        )

    def n_all():
        ref = norms.at[pl.ds(0, NDP - 1)]
        return pltpu.make_async_remote_copy(
            src_ref=ref, dst_ref=ref, send_sem=n_s, recv_sem=n_r,
            device_id=(other, p), device_id_type=MESH,
        )

    @pl.loop(1, NPREC)
    def _(i):
        b_copy(lax.rem(p + i, NPREC), p).start()

    got[p] = slots[pl.ds(SL * p, SL)]

    ring_start(wall, RR, RD, 2)

    norm[...] = jnp.zeros_like(norm)

    def own_strip(s):
        rows = got[:, s].astype(F32).reshape(NPREC * Q, LANES)
        strip_t[s] = rows
        square = jnp.sum(jnp.sum(rows * rows, axis=0, keepdims=True), axis=1, keepdims=True)
        norm[8 + s : 9 + s, :] = jnp.broadcast_to(square, (1, LANES))
        for c in range(8):
            for r in range(2):
                strip_m[c, pl.ds(r, NPREC, stride=2), :] = strip_t[
                    s, pl.ds(2 * c + r, NPREC, stride=Q), :
                ]
        for c in range(8):
            gall[s, d, :, c * LANES : (c + 1) * LANES] = strip_m[c].astype(BF)

    def whole_root(s, k):
        ring_other(wall, RD, s, k)
        for a in sorted({k, (NY - k) % NY}):
            strip = wall[s, pl.ds(2 * wrap(y + a), 2)].reshape(LANES, WIN * LANES)
            for w in range(WIN):
                b = (a + w) % NY
                block = strip[:, w * LANES : (w + 1) * LANES]
                rfull[s, a * LANES : (a + 1) * LANES, b * LANES : (b + 1) * LANES] = block
                if 0 < w < WIN - 1:
                    rfull[s, b * LANES : (b + 1) * LANES, a * LANES : (a + 1) * LANES] = block.T

    def chips(k):
        return [wrap(y + k)] if k in (0, 4) else [wrap(y + k), wrap(y - k)]

    def chip_rows(s, k):
        return jnp.concatenate(
            [gall[s, pl.ds(2 * c, 2)].reshape(LANES, ORDER) for c in chips(k)], axis=0
        )

    def add_products(s, k):
        lhs = []
        for c in chips(k):
            here = pl.ds(pl.multiple_of(c * LANES, LANES), LANES)
            mine = pl.ds(pl.multiple_of(y * LANES, LANES), LANES)
            cols = gall[s, pl.ds(2 * c, 2), :, mine].reshape(LANES, LANES).T
            cols = jnp.where(core == 0, cols[:STRIP], cols[STRIP:])
            lhs.append(jnp.concatenate([lroot[s, :, here], cols], axis=0))
        lhs = jnp.concatenate(lhs, axis=1)
        rhs = chip_rows(s, k)
        for n in range(ORDER // TILE):
            tile = slice(n * TILE, (n + 1) * TILE)
            res = jnp.dot(lhs, rhs[:, tile], preferred_element_type=F32)
            if k == 0:
                half_acc[s, :, tile] = res[:STRIP]
                right_out[s, :, tile] = res[STRIP:]
            elif k < 4:
                half_acc[s, :, tile] += res[:STRIP]
                right_out[s, :, tile] += res[STRIP:]
            else:
                half[:, tile] = (half_acc[s, :, tile] + res[:STRIP]).astype(BF)
                right_out[s, :, tile] += res[STRIP:]

    def left_product(s, k):
        res = lax.dot_general(
            gall[s, d], chip_rows(s, k), (((1,), (1,)), ((), ())), preferred_element_type=F32
        )
        for j, c in enumerate(chips(k)):
            here = pl.ds(pl.multiple_of(c * LANES, LANES), LANES)
            left_out[s, :, here] = res[:, j * LANES : (j + 1) * LANES]

    def precondition(s):
        square = jnp.zeros((1, TILE), F32)
        near = [wrap(y + a) for a in range(NY)]
        lhs = jnp.concatenate(
            [half[:, pl.ds(pl.multiple_of(c * LANES, LANES), LANES)] for c in near], axis=1
        )
        for n in range(ORDER // TILE):
            tile = slice(n * TILE, (n + 1) * TILE)
            pre = jnp.dot(lhs, rfull[s, :, tile], preferred_element_type=F32)
            square += jnp.sum(pre * pre, axis=0, keepdims=True)
            for h in range(TILE // LANES):
                prec_m[near[n * (TILE // LANES) + h]] = pre[:, h * LANES : (h + 1) * LANES]
        norm[s : s + 1, :] = jnp.broadcast_to(jnp.sum(square, axis=1, keepdims=True), (1, LANES))

    def send_norms():
        @pl.loop(1, NDP)
        def _(i):
            n_copy(lax.rem(d + i, NDP), d).start()

        norms[d] = norm[...]

    def send_rows(s):
        for c in range(8):
            for r in range(2):
                strip_t[s, pl.ds(2 * c + r, NPREC, stride=Q), :] = prec_m[
                    c, pl.ds(r, NPREC, stride=2), :
                ]
        outgo[s] = strip_t[s].astype(BF).reshape(NPREC, Q, LANES)

        @pl.loop(1, NPREC)
        def _(i):
            e_copy(s, lax.rem(p + i, NPREC), p).start()

        back[SL * p + s] = outgo[s, p]

    def f_copy(to, fro):
        return pltpu.make_async_remote_copy(
            src_ref=fac,
            dst_ref=facs.at[fro],
            send_sem=f_s,
            recv_sem=f_r,
            device_id=(d, to),
            device_id_type=MESH,
        )

    def f_all():
        ref = facs.at[pl.ds(0, NPREC - 1)]
        return pltpu.make_async_remote_copy(
            src_ref=ref, dst_ref=ref, send_sem=f_s, recv_sem=f_r,
            device_id=(other, p), device_id_type=MESH,
        )

    def out_copies(s):
        return [
            pltpu.make_async_copy(left_out.at[s], left_hbm.at[s], out_sem.at[0, s]),
            pltpu.make_async_copy(right_out.at[s], right_hbm.at[s], out_sem.at[1, s]),
        ]

    def grams(s, k):
        ring_other(gall, GD, s, k)
        add_products(s, k)
        left_product(s, k)

    def step(s, k):
        ring_step(gall, GR, GD, s, k)

    def finish(s):
        ring_other(gall, GD, s, 4)
        add_products(s, 4)
        precondition(s)
        if s == SL - 1:
            send_norms()
        send_rows(s)
        left_product(s, 4)
        for copy in out_copies(s):
            copy.start()

    for s in range(SL):
        ring_step(wall, RR, RD, s, 1)
        whole_root(s, 0)
    for s in range(SL):
        ring_step(wall, RR, RD, s, 2)
        whole_root(s, 1)
    ring_step(wall, RR, RD, 0, 3)
    whole_root(0, 2)
    b_all().wait_recv()
    own_strip(0)
    ring_start(gall, GR, GD, 0)
    ring_step(wall, RR, RD, 1, 3)
    ring_step(wall, RR, RD, 2, 3)
    own_strip(1)
    ring_start(gall, GR, GD, 1)
    whole_root(1, 2)
    own_strip(2)
    whole_root(2, 2)
    whole_root(0, 3)
    step(0, 1)
    whole_root(1, 3)
    for s in range(SL):
        ring_step(wall, RR, RD, s, 4)
    grams(0, 0)
    whole_root(2, 3)
    step(1, 1)
    grams(1, 0)
    step(0, 2)
    whole_root(0, 4)
    grams(0, 1)
    ring_start(gall, GR, GD, 2)
    grams(1, 1)
    step(1, 2)
    grams(0, 2)
    step(0, 3)
    whole_root(1, 4)
    grams(2, 0)
    grams(1, 2)
    step(2, 1)
    grams(0, 3)
    step(1, 3)
    step(0, 4)
    grams(2, 1)
    finish(0)
    step(2, 2)
    grams(1, 3)
    step(1, 4)
    grams(2, 2)
    step(2, 3)
    finish(1)
    whole_root(2, 4)
    grams(2, 3)
    step(2, 4)
    finish(2)
    n_all().wait_recv()
    total = jnp.sum(norms[...], axis=0)
    fac[...] = jnp.sqrt(total[8:16]) / (jnp.sqrt(total[0:8]) + 1e-06)

    @pl.loop(1, NPREC)
    def _(i):
        f_copy(lax.rem(p + i, NPREC), p).start()

    facs[p] = fac[...]

    for s in range(SL):
        ring_drain(wall, RR, RD, s)
        ring_drain(gall, GR, GD, s)
    for g in range(2):
        for t in range(5):
            sib_part(g, t).wait_send()
        for t in range(4):
            for h in range(2):
                if t or h == g:
                    rs_copy(g, t, h).wait_send()
    b_all().wait_send()
    n_all().wait_send()
    for s in range(SL):
        e_all(s).wait_send()
        e_all(s).wait_recv()
    f_all().wait_send()
    f_all().wait_recv()

    @pl.loop(0, NB, unroll=8)
    def _(b):
        slot = table[b]
        scale = facs[lax.div(slot, SL), pl.ds(lax.rem(slot, SL), 1), :]
        upd_out[b] = (back[slot].astype(F32) * scale).astype(BF)

    last = pltpu.make_async_copy(upd_out, upd_hbm, out_sem.at[2, 0])
    last.start()
    for s in range(SL):
        for copy in out_copies(s):
            copy.wait()
    last.wait()


def hand_over(left_in, right_in, upd_in, left, right, upd, a, b, c, sem_in, sem_out):
    ins, outs = [], []
    for s in range(SL):
        for n, (src, mid, dst) in enumerate(((left_in, a, left), (right_in, b, right))):
            ins.append(pltpu.make_async_copy(src.at[s], mid.at[s], sem_in.at[n, s]))
            outs.append(pltpu.make_async_copy(mid.at[s], dst.at[s], sem_out.at[n, s]))
    ins.append(pltpu.make_async_copy(upd_in, c, sem_in.at[2, 0]))
    outs.append(pltpu.make_async_copy(c, upd, sem_out.at[2, 0]))
    for copy in ins:
        copy.start()
    for arrive, leave in zip(ins, outs):
        arrive.wait()
        leave.start()
    for copy in outs:
        copy.wait()


def body(grad_part, table, left_root, right_root):
    grad = grad_part.reshape(NB, NDP, 2, 8, LANES).transpose(0, 1, 3, 2, 4)
    grad = grad.reshape(NB, NDP, Q, LANES)
    slot = jnp.arange(SL * NPREC, dtype=jnp.int32)
    block = jnp.arange(1, NB + 1, dtype=jnp.int32)
    named = slot[:, None] == table[None, :]
    inv = jnp.sum(jnp.where(named, block[None, :], 0), axis=1, dtype=jnp.int32)
    vmem = pl.BlockSpec(memory_space=pltpu.VMEM)
    smem = pl.BlockSpec(memory_space=pltpu.SMEM)
    hbm = pl.BlockSpec(memory_space=pl.ANY)
    dma = pltpu.SemaphoreType.DMA
    results = [
        jax.ShapeDtypeStruct((SL, STRIP, ORDER), F32),
        jax.ShapeDtypeStruct((SL, STRIP, ORDER), F32),
        jax.ShapeDtypeStruct((NB, Q, LANES), BF),
    ]
    out = pl.pallas_call(
        kernel,
        out_shape=results,
        in_specs=[smem, smem, hbm, vmem, vmem],
        out_specs=[hbm, hbm, hbm],
        scratch_shapes=[
            pltpu.VMEM((NY, NB, Q, LANES), BF),
            pltpu.VMEM((NY, NB, Q, LANES), BF),
            pltpu.VMEM((2, 4, NB, Q, LANES), BF),
            pltpu.VMEM((NB + 1, Q, LANES), BF),
            pltpu.VMEM((SL * NPREC, Q, LANES), BF),
            pltpu.VMEM((NPREC, SL, Q, LANES), BF),
            pltpu.VMEM((SL, NPREC * Q, LANES), F32),
            pltpu.VMEM((8, STRIP, LANES), F32),
            pltpu.VMEM((SL, NDP, STRIP, ORDER), BF),
            pltpu.VMEM((SL, NDP, STRIP, WIN * LANES), BF),
            pltpu.VMEM((SL, ORDER, ORDER), BF),
            pltpu.VMEM((SL, STRIP, ORDER), F32),
            pltpu.VMEM((STRIP, ORDER), BF),
            pltpu.VMEM((8, STRIP, LANES), F32),
            pltpu.VMEM((SL, NPREC, Q, LANES), BF),
            pltpu.VMEM((SL * NPREC, Q, LANES), BF),
            pltpu.VMEM((16, LANES), F32),
            pltpu.VMEM((NDP, 16, LANES), F32),
            pltpu.VMEM((8, LANES), F32),
            pltpu.VMEM((NPREC, 8, LANES), F32),
            pltpu.VMEM((SL, STRIP, ORDER), F32),
            pltpu.VMEM((SL, STRIP, ORDER), F32),
            pltpu.VMEM((NB, Q, LANES), BF),
            dma((2, 5)), dma((2, 5)), dma((2, 5)),
            dma((2, 4, 2)), dma((2, 4, 2)),
            dma, dma,
            dma((SL, 2, 4, 2)), dma((SL, 2, 4, 2)), dma((SL, 9)), dma((SL, 9)),
            dma((SL, 2, 4, 2)), dma((SL, 2, 4, 2)), dma((SL, 9)), dma((SL, 9)),
            dma((SL,)), dma((SL,)),
            dma, dma,
            dma, dma,
            dma((3, SL)),
        ],
        compiler_params=pltpu.CompilerParams(
            collective_id=0, has_side_effects=True, vmem_limit_bytes=56 * 2**20
        ),
        cost_estimate=pl.CostEstimate(
            flops=2 * SL * 5 * STRIP * ORDER * ORDER, bytes_accessed=8 * 2**20, transcendentals=0
        ),
        name="shampoo_step",
    )(inv, table, grad, left_root, right_root)
    left, right, upd = pl.pallas_call(
        hand_over,
        out_shape=results,
        in_specs=[hbm, hbm, hbm],
        out_specs=[hbm, hbm, hbm],
        scratch_shapes=[
            pltpu.VMEM((SL, STRIP, ORDER), F32),
            pltpu.VMEM((SL, STRIP, ORDER), F32),
            pltpu.VMEM((NB, Q, LANES), BF),
            dma((3, SL)),
            dma((3, SL)),
        ],
        compiler_params=pltpu.CompilerParams(vmem_limit_bytes=56 * 2**20),
        name="hand_over",
    )(*out)
    update = upd.reshape(NB, 8, 2, LANES).transpose(0, 2, 1, 3).reshape(NB, 1, 1, 2, ORDER)
    return (left, right, update)


def solution(mesh):
    in_specs = (
        P("dp", None, None, "prec", None, None),
        P(),
        P("prec", "dp", None),
        P("prec", "dp", None),
    )
    out_specs = (P("prec", "dp", None), P("prec", "dp", None), P(None, "dp", "prec", None, None))
    return jax.shard_map(body, mesh=mesh, in_specs=in_specs, out_specs=out_specs, check_vma=False)
```
